512 devices in a mesh: depth: 16 (over z), lat: 32 (over x, y, core).
Axes of the slice: x: 4, y: 4, z: 16, core: 2. Of those that a mesh axis runs over, the one named last changes fastest.
Arguments:
- down_real: float32 [64, 256, 256], P('depth', 'lat'), may hold values from -6 to 6
- down_imaginary: float32 [64, 256, 256], P('depth', 'lat'), may hold values from -6 to 6
- up_real: float32 [64, 256, 256], P('depth', 'lat'), may hold values from -6 to 6
- up_imaginary: float32 [64, 256, 256], P('depth', 'lat'), may hold values from -6 to 6
- slowness: float32 [64, 256, 256], P('depth', 'lat'), may hold values from 0.7 to 1.4
- ref_slow: float32 [64], P('depth'), may hold values from 0.8 to 1.2
- reflectivity: float32 [64, 256, 256], P('depth', 'lat'), may hold values from -0.3 to 0.3
- source_real: float32 [256, 256], P('lat'), may hold values from -6 to 6
- source_imaginary: float32 [256, 256], P('lat'), may hold values from -6 to 6
Outputs:
- next_down_real: float32 [64, 256, 256], P('depth', 'lat')
- next_down_imaginary: float32 [64, 256, 256], P('depth', 'lat')
- next_up_real: float32 [64, 256, 256], P('depth', 'lat')
- next_up_imaginary: float32 [64, 256, 256], P('depth', 'lat')
The draws below stay inside these ranges and needn't reach their ends.
All inputs are finite; a program needn't handle non-finite values.
Results may differ from the reference program's by a relative error of at most 0.0003.
Values sent between devices are 32-bit elements; how exact they have to be, the bound alone decides.
A program may use at most 64 MiB of HBM per device.

```python
import math
import jax
import jax.numpy as jnp
from jax import lax

NX = 256
NY = 256
TICKS = 3
NZ = 64


def block_levels(stream_key, dims, pieces, low, high):
    gain, own = 1.0, jax.random.fold_in(stream_key, 6)
    for dim, parts in pieces:
        steps = jnp.exp(jax.random.uniform(jax.random.fold_in(own, dim), (parts,), jnp.float32, low / len(pieces), high / len(pieces)))
        gain = gain * jnp.repeat(steps, dims[dim] // parts).reshape([-1 if axis == dim else 1 for axis in range(len(dims))])
    return gain


def bell_draw(stream_key, dims, spread, bound, cuts=(), kind=jnp.bfloat16):
    result = spread * jax.random.normal(stream_key, dims, jnp.float32)
    if cuts:
        result = result * block_levels(stream_key, dims, cuts, -0.22, 0.18)
    return jnp.clip(result, -bound, bound).astype(kind)


def setup_inputs(seed: int = 0) -> dict:
    key_list = jax.random.split(jax.random.key(seed), 10)
    return {
        "down_real": bell_draw(key_list[0], (NZ, NX, NY), 1.0, 6.0, ((0, 16), (1, 32)), jnp.float32),
        "down_imaginary": bell_draw(key_list[1], (NZ, NX, NY), 1.0, 6.0, ((0, 16), (1, 32)), jnp.float32),
        "up_real": bell_draw(key_list[2], (NZ, NX, NY), 1.0, 6.0, ((0, 16), (1, 32)), jnp.float32),
        "up_imaginary": bell_draw(key_list[3], (NZ, NX, NY), 1.0, 6.0, ((0, 16), (1, 32)), jnp.float32),
        "slowness": jnp.clip(0.7 + 0.7 * jax.random.uniform(key_list[4], (NZ, NX, NY), jnp.float32) ** block_levels(key_list[4], (NZ, NX, NY), ((0, 16), (1, 32)), -0.2, 0.2), 0.7, 1.4),
        "ref_slow": jnp.clip(0.8 + 0.40000004 * jax.random.uniform(key_list[5], (NZ,), jnp.float32) ** block_levels(key_list[5], (NZ,), ((0, 16),), -0.2, 0.2), 0.8, 1.2),
        "reflectivity": jnp.clip(jax.random.uniform(key_list[6], (NZ, NX, NY), jnp.float32, -0.3, 0.3) * block_levels(key_list[6], (NZ, NX, NY), ((0, 16), (1, 32)), -0.4, 0.0), -0.3, 0.3),
        "source_real": bell_draw(key_list[7], (NX, NY), 1.0, 6.0, ((0, 32),), jnp.float32),
        "source_imaginary": bell_draw(key_list[8], (NX, NY), 1.0, 6.0, ((0, 32),), jnp.float32),
    }


OMEGA = 2.5
DEPTH_STEP = 1.0

def wavenumbers(count):
    index = jnp.arange(count, dtype=jnp.int32)
    wrapped = jnp.where(index < count // 2, index, index - count)
    return wrapped.astype(jnp.float32) * (2.0 * math.pi / count)

def propagate(real, imag, slowness, ref_slow):
    wave_x = wavenumbers(NX)
    wave_y = wavenumbers(NY)
    squared = wave_x[:, None] ** 2 + wave_y[None, :] ** 2

    def one_level(items):
        plane_real, plane_imag, slow_plane, slow_ref = items
        plane = plane_real + 1j * plane_imag
        spectrum = jnp.fft.fft2(plane)
        argument = (OMEGA * slow_ref) ** 2 - squared
        vertical = jnp.sqrt(jnp.maximum(argument, 0.0)) * DEPTH_STEP
        evanescent = jnp.sqrt(jnp.maximum(-argument, 0.0)) * DEPTH_STEP
        factor = jnp.exp(-evanescent)
        multiplier = factor * jnp.cos(vertical) - 1j * (factor * jnp.sin(vertical))
        shifted = jnp.fft.ifft2(spectrum * multiplier)
        theta = OMEGA * (slow_plane - slow_ref) * DEPTH_STEP
        corrected = shifted * (jnp.cos(theta) - 1j * jnp.sin(theta))
        return (jnp.real(corrected), jnp.imag(corrected))
    return lax.map(one_level, (real, imag, slowness, ref_slow))

def reference(down_real, down_imaginary, up_real, up_imaginary, slowness, ref_slow, reflectivity, source_real, source_imaginary):
    for tick in range(TICKS):
        prop_down_real, prop_down_imag = propagate(down_real, down_imaginary, slowness, ref_slow)
        prop_up_real, prop_up_imag = propagate(up_real, up_imaginary, slowness, ref_slow)
        in_down_real = jnp.concatenate([source_real[None], prop_down_real[:-1]], axis=0)
        in_down_imag = jnp.concatenate([source_imaginary[None], prop_down_imag[:-1]], axis=0)
        in_up_real = jnp.concatenate([prop_up_real[1:], jnp.zeros_like(prop_up_real[:1])], axis=0)
        in_up_imag = jnp.concatenate([prop_up_imag[1:], jnp.zeros_like(prop_up_imag[:1])], axis=0)
        down_real = in_down_real - reflectivity * in_up_real
        down_imaginary = in_down_imag - reflectivity * in_up_imag
        up_real = in_up_real + reflectivity * in_down_real
        up_imaginary = in_up_imag + reflectivity * in_down_imag
    return (down_real, down_imaginary, up_real, up_imaginary)
```

```python
import math

import jax
import jax.numpy as jnp
import ml_dtypes
import numpy as np
from jax import lax
from jax.experimental import pallas as pl
from jax.experimental.pallas import tpu as pltpu
from jax.sharding import PartitionSpec as P

TICKS = 3
OMEGA = 2.5
MESH = pl.DeviceIdType.MESH

LEVELS = 4
PLANES = 2 * LEVELS
LAT = 32
ROWS = 8
N = 256
LANES = 2 * PLANES * ROWS
HALF = LANES // 2


def split(x):
    high = x.astype(jnp.bfloat16)
    low = (x - high.astype(jnp.float32)).astype(jnp.bfloat16)
    return high, low


def np_split(x):
    x = np.asarray(x, np.float64)
    high = x.astype(np.float32).astype(ml_dtypes.bfloat16)
    low = (x - high.astype(np.float64)).astype(np.float32).astype(ml_dtypes.bfloat16)
    return high, low


def constants():
    index = np.arange(N)
    angle = 2.0 * np.pi * (np.outer(index, index) % N) / N
    cos_hi, cos_lo = np_split(np.cos(angle))
    sin_hi, sin_lo = np_split(np.sin(angle))
    full = np.stack([cos_hi, sin_hi, cos_lo, sin_lo])
    coarse = np.arange(LAT)
    angle = 2.0 * np.pi * (np.outer(coarse, coarse) % LAT) / LAT
    eye = np.eye(ROWS)
    both = np.concatenate([np.kron(np.cos(angle), eye), np.kron(np.sin(angle), eye)])
    outer = np.stack(np_split(both))
    fine = np.arange(ROWS)
    angle = 2.0 * np.pi * (np.outer(fine, fine) % ROWS) / ROWS
    cosine, sine = (np.kron(np.eye(PLANES), f(angle)) for f in (np.cos, np.sin))
    inner = []
    for sign in (1.0, -1.0):
        block = np.block([[cosine, -sign * sine], [sign * sine, cosine]])
        high, low = np_split(block)
        inner.append(np.block([[high, low], [high, low]]))
    inner = np.stack(inner)
    turn = 2.0 * np.pi * np.outer(coarse, fine) / N
    cosine = np.tile(np.cos(turn), (1, LANES // ROWS))
    sine = np.tile(np.sin(turn), (1, LANES // ROWS))
    sine[:, HALF:] *= -1.0
    twiddle = np.stack([cosine, sine]).astype(np.float32)[:, :, None, :]
    return full, outer, inner, twiddle


def dot(a, b, dims=((1,), (0,))):
    return lax.dot_general(a, b, (dims, ((), ())), preferred_element_type=jnp.float32)


def forward_y(real, imag, full):
    real_hi, real_lo = split(real)
    imag_hi, imag_lo = split(imag)
    same = jnp.concatenate([real_hi, imag_hi, real_lo, imag_lo], axis=0)
    swapped = jnp.concatenate([imag_hi, -real_hi, imag_lo, -real_lo], axis=0)
    last = ((1,), (1,))
    wide = dot(full[0], same, last) + dot(full[1], swapped, last)
    rest = dot(full[2], same[:LANES], last) + dot(full[3], swapped[:LANES], last)
    return wide[:, :LANES] + (wide[:, LANES:] + rest)


def signs(shape):
    lane = lax.broadcasted_iota(jnp.int32, shape, len(shape) - 1)
    return jnp.where(lane < HALF, 1.0, -1.0).astype(jnp.float32)


def outer_step(x, outer, sign, roll):
    high, low = split(x)
    wide = dot(outer[0], jnp.concatenate([high, low], axis=1))
    total = wide[:, :LANES] + (wide[:, LANES:] + dot(outer[1], high))
    return total[:N] + sign * roll(total[N:])


def inner_step(x, inner):
    high, low = split(x)
    wide = dot(jnp.concatenate([high, low], axis=1), inner)
    return wide[:, :LANES] + wide[:, LANES:]


def turned(x, cosine, sine, roll):
    return x * cosine + roll(x) * sine


def middle(x, mult_real, mult_imag, outer, inner, twiddle, roll):
    sign = signs((N, LANES))
    shape = (LAT, ROWS, LANES)
    cosine = jnp.broadcast_to(twiddle[0], shape).reshape(N, LANES)
    sine = jnp.broadcast_to(twiddle[1], shape).reshape(N, LANES)
    x = outer_step(x, outer, sign, roll)
    x = turned(x, cosine, sine, roll)
    x = inner_step(x, inner[0])
    x = turned(x, mult_real, mult_imag, roll)
    x = inner_step(x, inner[1])
    x = turned(x, cosine, -sine, roll)
    return outer_step(x, outer, -sign, roll)


def backward_y(x, full):
    high, low = split(x.T)
    both = jnp.concatenate([high, low], axis=0)
    cosine = dot(both, full[0])
    sine = dot(both, full[1])
    cosine = cosine[:LANES] + (cosine[LANES:] + dot(high, full[2]))
    sine = sine[:LANES] + (sine[LANES:] + dot(high, full[3]))
    return cosine[:HALF] - sine[HALF:], cosine[HALF:] + sine[:HALF]


def wrapped_numbers(index):
    folded = jnp.where(index < N // 2, index, index - N)
    return folded.astype(jnp.float32) * (2.0 * math.pi / N)


def multiplier(me, ref_slow):
    row = lax.broadcasted_iota(jnp.int32, (N, LANES), 0)
    lane = lax.broadcasted_iota(jnp.int32, (N, LANES), 1)
    wave_x = wrapped_numbers(row // ROWS + LAT * (lane % ROWS))
    wave_y = wrapped_numbers(ROWS * me + row % ROWS)
    level = (lane // ROWS) % LEVELS
    slow = jnp.full((N, LANES), ref_slow[0], jnp.float32)
    for z in range(1, LEVELS):
        slow = jnp.where(level == z, ref_slow[z], slow)
    argument = (OMEGA * slow) ** 2 - (wave_x * wave_x + wave_y * wave_y)
    vertical = jnp.sqrt(jnp.maximum(argument, 0.0))
    factor = jnp.exp(-jnp.sqrt(jnp.maximum(-argument, 0.0))) * (1.0 / (N * N))
    return factor * jnp.cos(vertical), signs((N, LANES)) * (factor * jnp.sin(vertical))


def kernel(
    down_real, down_imag, up_real, up_imag, slowness, ref_slow, reflect, source_real, source_imag,
    full_hbm, outer_hbm, inner_hbm, twiddle_hbm,
    out_dr, out_di, out_ur, out_ui,
    state, slow, refl, source, full, outer, inner, twiddle,
    mult, corr, send_there, send_back, got_there, got_back, edge_send, edge_got,
    in_sems, out_sems, there_send, there_recv, back_send, back_recv, edge_send_sems, edge_recv_sems,
):
    me = lax.axis_index("lat")
    depth = lax.axis_index("depth")
    depths = lax.axis_size("depth")
    below = lax.rem(depth + 1, depths)
    above = lax.rem(depth + depths - 1, depths)

    def roll(x):
        return pltpu.roll(x, HALF, 1)

    loads = [
        pltpu.make_async_copy(src, dst, in_sems.at[n])
        for n, (src, dst) in enumerate([
            (down_real, state.at[0, 0]), (up_real, state.at[0, 1]),
            (down_imag, state.at[1, 0]), (up_imag, state.at[1, 1]),
            (full_hbm, full), (outer_hbm, outer), (inner_hbm, inner), (twiddle_hbm, twiddle),
            (slowness, slow), (reflect, refl), (source_real, source.at[0]), (source_imag, source.at[1]),
        ])
    ]
    for load in loads:
        load.start()

    barrier = pltpu.get_barrier_semaphore()

    def greet(step, _):
        pl.semaphore_signal(
            barrier, inc=1, device_id=(depth, lax.rem(me + step, LAT)), device_id_type=MESH
        )
        return 0

    lax.fori_loop(1, LAT, greet, 0)
    for neighbour in (above, below):
        pl.semaphore_signal(barrier, inc=1, device_id=(neighbour, me), device_id_type=MESH)
    for load in loads[:5]:
        load.wait()

    def exchange(tick, sent, got, send_sems, recv_sems):
        def send(step, _):
            peer = lax.rem(me + step, LAT)
            pltpu.make_async_remote_copy(
                src_ref=sent.at[tick, peer],
                dst_ref=got.at[tick, me],
                send_sem=send_sems.at[tick],
                recv_sem=recv_sems.at[tick],
                device_id=(depth, peer),
                device_id_type=MESH,
            ).start()
            return 0

        lax.fori_loop(1, LAT, send, 0)
        got[tick, me] = sent[tick, me]
        return pltpu.make_async_remote_copy(
            src_ref=sent.at[tick, pl.ds(0, LAT - 1)],
            dst_ref=got.at[tick, pl.ds(0, LAT - 1)],
            send_sem=send_sems.at[tick],
            recv_sem=recv_sems.at[tick],
            device_id=(depth, lax.rem(me + 1, LAT)),
            device_id_type=MESH,
        )

    def edge(tick, which, target):
        return pltpu.make_async_remote_copy(
            src_ref=edge_send.at[tick, which],
            dst_ref=edge_got.at[tick, which],
            send_sem=edge_send_sems.at[tick, which],
            recv_sem=edge_recv_sems.at[tick, which],
            device_id=(target, me),
            device_id_type=MESH,
        )

    def one_tick(tick, _):
        real = state[0].reshape(PLANES * ROWS, N)
        imag = state[1].reshape(PLANES * ROWS, N)
        send_there[tick] = forward_y(real, imag, full).reshape(LAT, ROWS, LANES)

        @pl.when(tick == 0)
        def _():
            pl.semaphore_wait(barrier, LAT + 1)

        there = exchange(tick, send_there, got_there, there_send, there_recv)

        @pl.when(tick == 0)
        def _():
            for load in loads[5:]:
                load.wait()
            mult[0], mult[1] = multiplier(me, ref_slow)

        there.wait_recv()
        x = got_there[tick].reshape(N, LANES)
        x = middle(x, mult[0], mult[1], outer, inner, twiddle, roll)
        send_back[tick] = x.reshape(LAT, ROWS, LANES)
        back = exchange(tick, send_back, got_back, back_send, back_recv)

        @pl.when(tick == 0)
        def _():
            for z in range(LEVELS):
                theta = OMEGA * (slow[z] - ref_slow[z])
                corr[0, z] = jnp.cos(theta)
                corr[1, z] = jnp.sin(theta)

        back.wait_recv()
        real, imag = backward_y(got_back[tick].reshape(N, LANES), full)
        real = real.reshape(2, LEVELS, ROWS, N)
        imag = imag.reshape(2, LEVELS, ROWS, N)
        prop_real = real * corr[0] + imag * corr[1]
        prop_imag = imag * corr[0] - real * corr[1]
        edge_send[tick, 0, 0] = prop_real[0, LEVELS - 1]
        edge_send[tick, 0, 1] = prop_imag[0, LEVELS - 1]
        edge_send[tick, 1, 0] = prop_real[1, 0]
        edge_send[tick, 1, 1] = prop_imag[1, 0]
        edges = [edge(tick, 0, below), edge(tick, 1, above)]
        for one in edges:
            one.start()
        is_top = depth == 0
        is_bottom = depth == depths - 1
        for part, prop in enumerate((prop_real, prop_imag)):
            for z in range(1, LEVELS - 1):
                state[part, 0, z] = prop[0, z - 1] - refl[z] * prop[1, z + 1]
                state[part, 1, z] = prop[1, z + 1] + refl[z] * prop[0, z - 1]
        for one in edges:
            one.wait_recv()
        last = LEVELS - 1
        for part, prop in enumerate((prop_real, prop_imag)):
            head = jnp.where(is_top, source[part], edge_got[tick, 0, part])
            tail = jnp.where(is_bottom, 0.0, edge_got[tick, 1, part])
            state[part, 0, 0] = head - refl[0] * prop[1, 1]
            state[part, 1, 0] = prop[1, 1] + refl[0] * head
            state[part, 0, last] = prop[0, last - 1] - refl[last] * tail
            state[part, 1, last] = tail + refl[last] * prop[0, last - 1]
        there.wait_send()
        back.wait_send()
        for one in edges:
            one.wait_send()
        return 0

    lax.fori_loop(0, TICKS, one_tick, 0)
    stores = [
        pltpu.make_async_copy(src, dst, out_sems.at[n])
        for n, (src, dst) in enumerate([
            (state.at[0, 0], out_dr), (state.at[1, 0], out_di),
            (state.at[0, 1], out_ur), (state.at[1, 1], out_ui),
        ])
    ]
    for store in stores:
        store.start()
    for store in stores:
        store.wait()


def solution(mesh):
    consts = constants()
    plane = jax.ShapeDtypeStruct((LEVELS, ROWS, N), jnp.float32)
    anywhere = pl.BlockSpec(memory_space=pl.ANY)
    smem = pl.BlockSpec(memory_space=pltpu.SMEM)
    f32 = jnp.float32

    def step(*args):
        return pl.pallas_call(
            kernel,
            out_shape=[plane] * 4,
            in_specs=[anywhere] * 5 + [smem] + [anywhere] * 7,
            out_specs=[anywhere] * 4,
            scratch_shapes=[
                pltpu.VMEM((2, 2, LEVELS, ROWS, N), f32),
                pltpu.VMEM((LEVELS, ROWS, N), f32),
                pltpu.VMEM((LEVELS, ROWS, N), f32),
                pltpu.VMEM((2, ROWS, N), f32),
                *[pltpu.VMEM(c.shape, c.dtype) for c in consts],
                pltpu.VMEM((2, N, LANES), f32),
                pltpu.VMEM((2, LEVELS, ROWS, N), f32),
                *[pltpu.VMEM((TICKS, LAT, ROWS, LANES), f32)] * 4,
                *[pltpu.VMEM((TICKS, 2, 2, ROWS, N), f32)] * 2,
                pltpu.SemaphoreType.DMA((12,)),
                pltpu.SemaphoreType.DMA((4,)),
                *[pltpu.SemaphoreType.DMA((TICKS,))] * 4,
                *[pltpu.SemaphoreType.DMA((TICKS, 2))] * 2,
            ],
            compiler_params=pltpu.CompilerParams(
                collective_id=0, has_side_effects=True, vmem_limit_bytes=32 * 2**20
            ),
        )(*args, *[jnp.asarray(c) for c in consts])

    lateral = P("depth", "lat", None)
    return jax.shard_map(
        step,
        mesh=mesh,
        in_specs=(lateral,) * 5 + (P("depth"), lateral, P("lat", None), P("lat", None)),
        out_specs=(lateral,) * 4,
        check_vma=False,
    )
```

```python
import math

import jax
import jax.numpy as jnp
import ml_dtypes
import numpy as np
from jax import lax
from jax.experimental import pallas as pl
from jax.experimental.pallas import tpu as pltpu
from jax.sharding import PartitionSpec as P

TICKS = 3
OMEGA = 2.5
MESH = pl.DeviceIdType.MESH

LEVELS = 4
GROUP = 8
LAT = 32
ROWS = 8
N = 256
LANES = 128
HALF = 64
SLOT = 16


def split(x):
    high = x.astype(jnp.bfloat16)
    low = (x - high.astype(jnp.float32)).astype(jnp.bfloat16)
    return high, low


def np_split(x):
    x = np.asarray(x, np.float64)
    high = x.astype(np.float32).astype(ml_dtypes.bfloat16)
    low = (x - high.astype(np.float64)).astype(np.float32).astype(ml_dtypes.bfloat16)
    return high, low


def constants():
    index = np.arange(N)
    slot, device, row = np.meshgrid(np.arange(LEVELS), np.arange(GROUP), np.arange(ROWS), indexing="ij")
    waves = (LAT * device + ROWS * slot + row).reshape(-1)
    angle = 2.0 * np.pi * (np.outer(waves, index) % N) / N
    cos_hi, cos_lo = np_split(np.cos(angle))
    sin_hi, sin_lo = np_split(np.sin(angle))
    full = np.stack([cos_hi, sin_hi, cos_lo, sin_lo])
    coarse = np.arange(LAT)
    angle = 2.0 * np.pi * (np.outer(coarse, coarse) % LAT) / LAT
    eye = np.eye(ROWS)
    both = np.concatenate([np.kron(np.cos(angle), eye), np.kron(np.sin(angle), eye)])
    outer = np.stack(np_split(both))
    fine = np.arange(ROWS)
    angle = 2.0 * np.pi * (np.outer(fine, fine) % ROWS) / ROWS
    cosine, sine = (np.kron(np.eye(HALF // ROWS), f(angle)) for f in (np.cos, np.sin))
    inner = []
    for sign in (1.0, -1.0):
        block = np.block([[cosine, -sign * sine], [sign * sine, cosine]])
        high, low = np_split(block)
        inner.append(np.block([[high, low], [high, low]]))
    inner = np.stack(inner)
    turn = 2.0 * np.pi * np.outer(coarse, fine) / N
    cosine = np.tile(np.cos(turn), (1, LANES // ROWS))
    sine = np.tile(np.sin(turn), (1, LANES // ROWS))
    sine[:, HALF:] *= -1.0
    twiddle = np.stack([cosine, sine]).astype(np.float32)[:, :, None, :]
    return full, outer, inner, twiddle


def dot(a, b, dims=((1,), (0,))):
    return lax.dot_general(a, b, (dims, ((), ())), preferred_element_type=jnp.float32)


def lanes(shape):
    return lax.broadcasted_iota(jnp.int32, shape, len(shape) - 1)


def slot_swap(tiles, roll):
    slot = (lanes(tiles[0].shape) // SLOT) % LEVELS
    for bit in (2, 1):
        keep = (slot & bit) == 0
        shift = bit * SLOT
        new = list(tiles)
        for a in range(LEVELS):
            if a & bit == 0:
                low, high = tiles[a], tiles[a + bit]
                new[a] = jnp.where(keep, low, roll(high, shift))
                new[a + bit] = jnp.where(keep, roll(low, LANES - shift), high)
        tiles = new
    return tiles


def forward_y(real, imag, full, roll):
    real_hi, real_lo = split(real)
    imag_hi, imag_lo = split(imag)
    same = jnp.concatenate([real_hi, imag_hi, real_lo, imag_lo], axis=0)
    swapped = jnp.concatenate([imag_hi, -real_hi, imag_lo, -real_lo], axis=0)
    last = ((1,), (1,))
    wide = dot(full[0], same, last) + dot(full[1], swapped, last)
    rest = dot(full[2], same[:LANES], last) + dot(full[3], swapped[:LANES], last)
    total = wide[:, :LANES] + (wide[:, LANES:] + rest)
    return slot_swap([total[HALF * a : HALF * (a + 1)] for a in range(LEVELS)], roll)


def signs(shape):
    return jnp.where(lanes(shape) < HALF, 1.0, -1.0).astype(jnp.float32)


def outer_step(x, outer, sign, roll):
    high, low = split(x)
    wide = dot(outer[0], jnp.concatenate([high, low], axis=1))
    total = wide[:, :LANES] + (wide[:, LANES:] + dot(outer[1], high))
    return total[:N] + sign * roll(total[N:], HALF)


def inner_step(x, inner):
    high, low = split(x)
    wide = dot(jnp.concatenate([high, low], axis=1), inner)
    return wide[:, :LANES] + wide[:, LANES:]


def turned(x, cosine, sine, roll):
    return x * cosine + roll(x, HALF) * sine


def middle(x, mult_real, mult_imag, outer, inner, twiddle, roll):
    sign = signs((N, LANES))
    shape = (LAT, ROWS, LANES)
    cosine = jnp.broadcast_to(twiddle[0], shape).reshape(N, LANES)
    sine = jnp.broadcast_to(twiddle[1], shape).reshape(N, LANES)
    x = outer_step(x, outer, sign, roll)
    x = turned(x, cosine, sine, roll)
    x = inner_step(x, inner[0])
    x = turned(x, mult_real, mult_imag, roll)
    x = inner_step(x, inner[1])
    x = turned(x, cosine, -sine, roll)
    return outer_step(x, outer, -sign, roll)


def is_down(shape):
    return (lanes(shape) // ROWS) % 2 == 0


def packed(even, odd, roll):
    down = is_down(even.shape)
    return jnp.where(down, even, roll(odd, ROWS)), jnp.where(down, roll(even, LANES - ROWS), odd)


def backward_y(tiles, full, roll):
    x = jnp.concatenate(slot_swap(tiles, roll), axis=0)
    high, low = split(x.T)
    both = jnp.concatenate([high, low], axis=0)
    cosine = dot(both, full[0])
    sine = dot(both, full[1])
    cosine = cosine[:LANES] + (cosine[LANES:] + dot(high, full[2]))
    sine = sine[:LANES] + (sine[LANES:] + dot(high, full[3]))
    return cosine[:HALF] - sine[HALF:], cosine[HALF:] + sine[:HALF]


def wrapped_numbers(index):
    folded = jnp.where(index < N // 2, index, index - N)
    return folded.astype(jnp.float32) * (2.0 * math.pi / N)


def multiplier(member, slow):
    row = lax.broadcasted_iota(jnp.int32, (N, LANES), 0)
    lane = lax.broadcasted_iota(jnp.int32, (N, LANES), 1)
    wave_x = wrapped_numbers(row // ROWS + LAT * (lane % ROWS))
    wave_y = wrapped_numbers(LAT * member + ROWS * ((lane // SLOT) % LEVELS) + row % ROWS)
    argument = (OMEGA * slow) ** 2 - (wave_x * wave_x + wave_y * wave_y)
    vertical = jnp.sqrt(jnp.maximum(argument, 0.0))
    factor = jnp.exp(-jnp.sqrt(jnp.maximum(-argument, 0.0))) * (1.0 / (N * N))
    return factor * jnp.cos(vertical), signs((N, LANES)) * (factor * jnp.sin(vertical))


def mixed(real, imag, corr, refl, heads, tails, source):
    out = []
    for part in range(2):
        if part == 0:
            prop = real * corr[0] + imag * corr[1]
        else:
            prop = imag * corr[0] - real * corr[1]
        down = jnp.where(heads, source[part], prop[0])
        up = jnp.where(tails, 0.0, prop[1])
        out.append((down - refl * up, up + refl * down))
    return out


def kernel(
    down_real, down_imag, up_real, up_imag, slowness, ref_slow, reflect, source_real, source_imag,
    full_hbm, outer_hbm, inner_hbm, twiddle_hbm,
    out_dr, out_di, out_ur, out_ui,
    state, slow, source, full, outer, inner, twiddle,
    mult, context, corr, sent_there, got_there, sent_back, got_back, got_last, tiles, edge_sent, edge_got,
    in_sems, out_sems, there_send, there_recv, back_send, back_recv, last_send, last_recv,
    edge_send, edge_recv, context_send, context_recv, source_send, source_recv,
):
    me = lax.axis_index("lat")
    depth = lax.axis_index("depth")
    depths = lax.axis_size("depth")
    member = lax.rem(me, GROUP)
    column = me // GROUP
    flipped = lax.rem(depth, 2)
    level = jnp.where(flipped == 1, LEVELS - 1 - column, column)
    has_above = depth > 0
    has_below = depth < depths - 1
    last = TICKS - 1

    def column_of(z):
        return jnp.where(flipped == 1, LEVELS - 1 - z, z)

    def roll(x, shift):
        return pltpu.roll(x, shift, x.ndim - 1)

    def remote(src, dst, send_sem, recv_sem, where):
        return pltpu.make_async_remote_copy(
            src_ref=src, dst_ref=dst, send_sem=send_sem, recv_sem=recv_sem,
            device_id=where, device_id_type=MESH,
        )

    neighbour = (depth, lax.bitwise_xor(me, 1))

    loads = [
        pltpu.make_async_copy(src, dst, in_sems.at[n])
        for n, (src, dst) in enumerate([
            (down_real, state.at[0, :, 0]), (up_real, state.at[0, :, 1]),
            (down_imag, state.at[1, :, 0]), (up_imag, state.at[1, :, 1]),
            (full_hbm, full), (outer_hbm, outer), (inner_hbm, inner), (twiddle_hbm, twiddle),
            (slowness, slow), (reflect, context.at[1, :, 2]),
            (source_real, source.at[0, 0]), (source_imag, source.at[0, 1]),
        ])
    ]
    for load in loads:
        load.start()

    barrier = pltpu.get_barrier_semaphore()

    def greet(step, _):
        pl.semaphore_signal(
            barrier, inc=1, device_id=(depth, lax.bitwise_xor(me, step)), device_id_type=MESH
        )
        return 0

    lax.fori_loop(1, LAT, greet, 0)

    @pl.when(has_above)
    def _():
        pl.semaphore_signal(barrier, inc=1, device_id=(depth - 1, me), device_id_type=MESH)

    @pl.when(has_below)
    def _():
        pl.semaphore_signal(barrier, inc=1, device_id=(depth + 1, me), device_id_type=MESH)

    for load in loads[:5]:
        load.wait()

    def first_there():
        pl.semaphore_wait(barrier, LAT - 1 + has_above.astype(jnp.int32) + has_below.astype(jnp.int32))

        def send(step, _):
            peer = lax.bitwise_xor(me, step)
            remote(
                sent_there.at[0, lax.rem(peer, GROUP), column_of(peer // GROUP)],
                got_there.at[0, me], there_send.at[0], there_recv.at[0], (depth, peer),
            ).start()
            return 0

        lax.fori_loop(1, LAT, send, 0)
        got_there[0, me] = sent_there[0, member, level]
        for load in loads[8:]:
            load.wait()
        for z in range(LEVELS):
            slow[z] = OMEGA * (slow[z] - ref_slow[z])
        edge_sent[0] = slow[LEVELS - 1]
        edge_sent[1] = slow[0]
        down = remote(edge_sent.at[0], edge_got.at[0], edge_send.at[0], edge_recv.at[0], (depth + 1, me))
        up = remote(edge_sent.at[1], edge_got.at[1], edge_send.at[1], edge_recv.at[1], (depth - 1, me))

        @pl.when(has_below)
        def _():
            down.start()

        @pl.when(has_above)
        def _():
            up.start()

        for z in range(LEVELS - 1):
            context[1, z + 1, 0] = slow[z]
            context[1, z, 1] = slow[z + 1]
        mine = ref_slow[0]
        for z in range(1, LEVELS):
            mine = jnp.where(level == z, ref_slow[z], mine)
        for load in loads[5:8]:
            load.wait()
        mult[0], mult[1] = multiplier(member, mine)
        nothing = jnp.zeros((ROWS, N), jnp.float32)

        @pl.when(has_above)
        def _():
            down.wait_recv()
            context[1, 0, 0] = edge_got[0]

        @pl.when(jnp.logical_not(has_above))
        def _():
            context[1, 0, 0] = nothing

        @pl.when(has_below)
        def _():
            up.wait_recv()
            context[1, LEVELS - 1, 1] = edge_got[1]

        @pl.when(jnp.logical_not(has_below))
        def _():
            context[1, LEVELS - 1, 1] = nothing

        holder = me // LEVELS
        place = lax.rem(me, LEVELS)
        for z in range(LEVELS):
            target = column_of(z) * GROUP + holder

            @pl.when(target != me)
            def _():
                remote(
                    context.at[1, z], context.at[0, place], context_send, context_recv, (depth, target)
                ).start()

            @pl.when(target == me)
            def _():
                context[0, place] = context[1, z]

        @pl.when(jnp.logical_not(has_above))
        def _():
            @pl.when(holder != me)
            def _():
                remote(
                    source.at[0], source.at[1 + place], source_send, source_recv, (depth, holder)
                ).start()

            @pl.when(holder == me)
            def _():
                source[1 + place] = source[0]

    def later_there(tick):
        def send(step, _):
            peer = lax.bitwise_xor(member, step)
            remote(
                sent_there.at[tick, peer], got_there.at[tick, pl.ds(LEVELS * member, LEVELS)],
                there_send.at[tick], there_recv.at[tick], (depth, column * GROUP + peer),
            ).start()
            return 0

        lax.fori_loop(1, GROUP, send, 0)
        got_there[tick, pl.ds(LEVELS * member, LEVELS)] = sent_there[tick, member]

    def group_back(tick):
        forth = jnp.where(flipped == 1, -1, 1)
        is_last = level == LEVELS - 1
        is_first = level == 0
        down_to = (
            depth + is_last.astype(jnp.int32), (column + jnp.where(is_last, 0, forth)) * GROUP,
        )
        up_to = (
            depth - is_first.astype(jnp.int32), (column - jnp.where(is_first, 0, forth)) * GROUP,
        )
        goes_down = jnp.logical_or(has_below, jnp.logical_not(is_last))
        goes_up = jnp.logical_or(has_above, jnp.logical_not(is_first))
        sides = ((0, goes_down, down_to), (1, goes_up, up_to))
        for side, goes, (to_depth, base) in sides:
            @pl.when(goes)
            def _():
                def send(step, _):
                    peer = lax.bitwise_xor(member, step)
                    remote(
                        sent_back.at[tick, pl.ds(LAT // 2 * side + 2 * peer, 2)],
                        got_back.at[tick, side, pl.ds(2 * member, 2)],
                        back_send.at[tick, side], back_recv.at[tick, side], (to_depth, base + peer),
                    ).start()
                    return 0

                lax.fori_loop(0, GROUP, send, 0)
        return sides

    def group_back_waits(tick, side):
        return remote(
            sent_back.at[tick, pl.ds(LAT // 2 * side, LAT // 2)], got_back.at[tick, side],
            back_send.at[tick, side], back_recv.at[tick, side], neighbour,
        )

    def last_waits(side, count, to):
        return remote(
            sent_back.at[last, pl.ds(0, count)], got_last.at[pl.ds(to, count)],
            last_send.at[side], last_recv.at[side], neighbour,
        )

    def one_tick(tick, _):
        real = state[0].reshape(HALF, N)
        imag = state[1].reshape(HALF, N)
        for g, x in enumerate(forward_y(real, imag, full, roll)):
            sent_there[tick, :, g] = x.reshape(GROUP, ROWS, LANES)

        @pl.when(tick == 0)
        def _():
            first_there()
            remote(
                got_there.at[0, pl.ds(0, LAT - 1)], got_there.at[0, pl.ds(0, LAT - 1)],
                there_send.at[0], there_recv.at[0], neighbour,
            ).wait_recv()

        @pl.when(tick > 0)
        def _():
            later_there(tick)
            remote(
                got_there.at[tick, pl.ds(0, LAT - LEVELS)],
                got_there.at[tick, pl.ds(0, LAT - LEVELS)],
                there_send.at[tick], there_recv.at[tick], neighbour,
            ).wait_recv()

        x = got_there[tick].reshape(N, LANES)
        x = middle(x, mult[0], mult[1], outer, inner, twiddle, roll).reshape(LAT, ROWS, LANES)

        @pl.when(tick < last)
        def _():
            pairs = x.reshape(LAT // 2, 2, ROWS, LANES)
            down, up = packed(pairs[:, 0], pairs[:, 1], roll)
            sent_back[tick, : LAT // 2] = down
            sent_back[tick, LAT // 2 :] = up
            sides = group_back(tick)

            def fill(which):
                angle = context[which, :, 0:2]
                corr[which, 0] = jnp.cos(angle)
                corr[which, 1] = jnp.sin(angle)

            @pl.when(tick == 0)
            def _():
                holder = member * LEVELS
                here = jnp.logical_and(me >= holder, me < holder + LEVELS)
                for count in (LEVELS - 1, LEVELS):
                    @pl.when(here == (count < LEVELS))
                    def _():
                        remote(
                            context.at[1, pl.ds(0, count)], context.at[0, pl.ds(0, count)],
                            context_send, context_recv, neighbour,
                        ).wait_recv()

                    @pl.when(jnp.logical_and(jnp.logical_not(has_above), column == 0))
                    def _():
                        @pl.when(here == (count < LEVELS))
                        def _():
                            remote(
                                source.at[pl.ds(0, count)], source.at[pl.ds(1, count)],
                                source_send, source_recv, neighbour,
                            ).wait_recv()

                fill(0)

            @pl.when(tick == 1)
            def _():
                fill(1)

            comes_down = jnp.logical_or(has_above, level > 0)
            comes_up = jnp.logical_or(has_below, level < LEVELS - 1)
            for side, comes in ((0, comes_down), (1, comes_up)):
                @pl.when(comes)
                def _():
                    group_back_waits(tick, side).wait_recv()

                @pl.when(jnp.logical_not(comes))
                def _():
                    got_back[tick, side] = jnp.zeros((LAT // 2, ROWS, LANES), jnp.float32)

            down = got_back[tick, 0].reshape(GROUP, 2, ROWS, LANES)
            up = got_back[tick, 1].reshape(GROUP, 2, ROWS, LANES)
            for j in range(2):
                tiles[2 * j], tiles[2 * j + 1] = packed(down[:, j], up[:, j], roll)
            for side, goes, _ in sides:
                @pl.when(goes)
                def _():
                    group_back_waits(tick, side).wait_send()

        @pl.when(tick == last)
        def _():
            sent_back[last] = x
            slot = level * GROUP + member

            def send(step, _):
                peer = lax.bitwise_xor(me, step)
                remote(
                    sent_back.at[last, peer], got_last.at[slot],
                    last_send.at[0], last_recv.at[0], (depth, peer),
                ).start()
                return 0

            def send_past(side, where, place):
                def send(step, _):
                    peer = lax.bitwise_xor(me, step)
                    remote(
                        sent_back.at[last, peer], got_last.at[place + member],
                        last_send.at[side], last_recv.at[side], (where, peer),
                    ).start()
                    return 0

                lax.fori_loop(0, LAT, send, 0)

            goes_down = jnp.logical_and(level == LEVELS - 1, has_below)
            goes_up = jnp.logical_and(level == 0, has_above)

            @pl.when(goes_down)
            def _():
                send_past(1, depth + 1, LAT)

            @pl.when(goes_up)
            def _():
                send_past(2, depth - 1, LAT + GROUP)

            lax.fori_loop(1, LAT, send, 0)
            got_last[slot] = sent_back[last, me]
            for side, comes, place in ((1, has_above, LAT), (2, has_below, LAT + GROUP)):
                @pl.when(comes)
                def _():
                    last_waits(side, GROUP, place).wait_recv()

                @pl.when(jnp.logical_not(comes))
                def _():
                    got_last[pl.ds(place, GROUP)] = jnp.zeros((GROUP, ROWS, LANES), jnp.float32)

            last_waits(0, LAT - 1, 0).wait_recv()
            down = is_down((GROUP, ROWS, LANES))
            for z in range(LEVELS):
                above = GROUP * (z - 1) if z > 0 else LAT
                below = GROUP * (z + 1) if z < LEVELS - 1 else LAT + GROUP
                tiles[z] = jnp.where(
                    down, got_last[above : above + GROUP], got_last[below : below + GROUP]
                )
            last_waits(0, LAT - 1, 0).wait_send()
            for side, goes in ((1, goes_down), (2, goes_up)):
                @pl.when(goes)
                def _():
                    last_waits(side, LAT, 0).wait_send()

        real, imag = backward_y([tiles[g].reshape(HALF, LANES) for g in range(LEVELS)], full, roll)
        real = real.reshape(LEVELS, 2, ROWS, N)
        imag = imag.reshape(LEVELS, 2, ROWS, N)
        at_end = (tick == last).astype(jnp.int32)
        for g in range(LEVELS):
            heads = jnp.logical_and(jnp.logical_not(has_above), jnp.where(tick == last, g, level) == 0)
            tails = jnp.logical_and(
                jnp.logical_not(has_below), jnp.where(tick == last, g, level) == LEVELS - 1
            )
            origin = source[jnp.where(tick == last, 0, 1 + g)]
            parts = mixed(
                real[g], imag[g], corr[at_end, :, g], context[at_end, g, 2], heads, tails, origin
            )
            for part in range(2):
                state[part, g, 0], state[part, g, 1] = parts[part]
        return 0

    lax.fori_loop(0, TICKS, one_tick, 0)
    stores = [
        pltpu.make_async_copy(src, dst, out_sems.at[n])
        for n, (src, dst) in enumerate([
            (state.at[0, :, 0], out_dr), (state.at[1, :, 0], out_di),
            (state.at[0, :, 1], out_ur), (state.at[1, :, 1], out_ui),
        ])
    ]
    for store in stores:
        store.start()

    remote(
        got_there.at[0, pl.ds(0, LAT - 1)], got_there.at[0, pl.ds(0, LAT - 1)],
        there_send.at[0], there_recv.at[0], neighbour,
    ).wait_send()
    for tick in range(1, TICKS):
        remote(
            got_there.at[tick, pl.ds(0, LAT - LEVELS)], got_there.at[tick, pl.ds(0, LAT - LEVELS)],
            there_send.at[tick], there_recv.at[tick], neighbour,
        ).wait_send()
    holder = me // LEVELS
    here = holder == member
    for count in (LEVELS - 1, LEVELS):
        @pl.when(here == (count < LEVELS))
        def _():
            remote(
                context.at[1, pl.ds(0, count)], context.at[0, pl.ds(0, count)],
                context_send, context_recv, neighbour,
            ).wait_send()

    @pl.when(jnp.logical_and(jnp.logical_not(has_above), holder != me))
    def _():
        remote(source.at[0], source.at[1], source_send, source_recv, neighbour).wait_send()

    for side, goes in ((0, has_below), (1, has_above)):
        @pl.when(goes)
        def _():
            remote(
                edge_sent.at[side], edge_got.at[side], edge_send.at[side], edge_recv.at[side], neighbour
            ).wait_send()

    for store in stores:
        store.wait()


def solution(mesh):
    consts = constants()
    plane = jax.ShapeDtypeStruct((LEVELS, ROWS, N), jnp.float32)
    anywhere = pl.BlockSpec(memory_space=pl.ANY)
    smem = pl.BlockSpec(memory_space=pltpu.SMEM)
    f32 = jnp.float32

    def step(*args):
        return pl.pallas_call(
            kernel,
            out_shape=[plane] * 4,
            in_specs=[anywhere] * 5 + [smem] + [anywhere] * 7,
            out_specs=[anywhere] * 4,
            scratch_shapes=[
                pltpu.VMEM((2, LEVELS, 2, ROWS, N), f32),
                pltpu.VMEM((LEVELS, ROWS, N), f32),
                pltpu.VMEM((1 + LEVELS, 2, ROWS, N), f32),
                *[pltpu.VMEM(c.shape, c.dtype) for c in consts],
                pltpu.VMEM((2, N, LANES), f32),
                pltpu.VMEM((2, LEVELS, 3, ROWS, N), f32),
                pltpu.VMEM((2, 2, LEVELS, 2, ROWS, N), f32),
                pltpu.VMEM((TICKS, GROUP, LEVELS, ROWS, LANES), f32),
                pltpu.VMEM((TICKS, LAT, ROWS, LANES), f32),
                pltpu.VMEM((TICKS, LAT, ROWS, LANES), f32),
                pltpu.VMEM((TICKS - 1, 2, LAT // 2, ROWS, LANES), f32),
                pltpu.VMEM((LAT + 2 * GROUP, ROWS, LANES), f32),
                pltpu.VMEM((LEVELS, GROUP, ROWS, LANES), f32),
                *[pltpu.VMEM((2, ROWS, N), f32)] * 2,
                pltpu.SemaphoreType.DMA((12,)),
                pltpu.SemaphoreType.DMA((4,)),
                *[pltpu.SemaphoreType.DMA((TICKS,))] * 2,
                *[pltpu.SemaphoreType.DMA((TICKS - 1, 2))] * 2,
                *[pltpu.SemaphoreType.DMA((3,))] * 2,
                *[pltpu.SemaphoreType.DMA((2,))] * 2,
                *[pltpu.SemaphoreType.DMA] * 4,
            ],
            compiler_params=pltpu.CompilerParams(collective_id=0, has_side_effects=True),
        )(*args, *[jnp.asarray(c) for c in consts])

    lateral = P("depth", "lat", None)
    return jax.shard_map(
        step,
        mesh=mesh,
        in_specs=(lateral,) * 5 + (P("depth"), lateral, P("lat", None), P("lat", None)),
        out_specs=(lateral,) * 4,
        check_vma=False,
    )
```

```python
import math

import jax
import jax.numpy as jnp
import ml_dtypes
import numpy as np
from jax import lax
from jax.experimental import pallas as pl
from jax.experimental.pallas import tpu as pltpu
from jax.sharding import PartitionSpec as P

TICKS = 3
OMEGA = 2.5
MESH = pl.DeviceIdType.MESH

LEVELS = 4
GROUP = 8
LAT = 32
FAR = 20
ROWS = 8
N = 256
LANES = 128
HALF = 64
WAVES = N // GROUP


def split(x):
    high = x.astype(jnp.bfloat16)
    low = (x - high.astype(jnp.float32)).astype(jnp.bfloat16)
    return high, low


def np_split(x):
    x = np.asarray(x, np.float64)
    high = x.astype(np.float32).astype(ml_dtypes.bfloat16)
    low = (x - high.astype(np.float64)).astype(np.float32).astype(ml_dtypes.bfloat16)
    return high, low


def constants():
    index = np.arange(N)
    angle = 2.0 * np.pi * (np.outer(index, index) % N) / N
    cos_hi, cos_lo = np_split(np.cos(angle))
    sin_hi, sin_lo = np_split(np.sin(angle))
    return np.stack([cos_hi, sin_hi, cos_lo, sin_lo])


def dot(a, b, dims=((1,), (0,))):
    return lax.dot_general(a, b, (dims, ((), ())), preferred_element_type=jnp.float32)


def lanes(shape):
    return lax.broadcasted_iota(jnp.int32, shape, len(shape) - 1)


def block_swap(tiles, roll):
    block = lanes(tiles[0].shape) // WAVES
    for bit in (2, 1):
        keep = (block & bit) == 0
        shift = bit * WAVES
        new = list(tiles)
        for a in range(4):
            if a & bit == 0:
                low, high = tiles[a], tiles[a + bit]
                new[a] = jnp.where(keep, low, roll(high, shift))
                new[a + bit] = jnp.where(keep, roll(low, LANES - shift), high)
        tiles = new
    return tiles


def along_y(real, imag, full, sign):
    real_hi, real_lo = split(real)
    imag_hi, imag_lo = split(imag)
    both = jnp.concatenate([real_hi, imag_hi, real_lo, imag_lo], axis=0)
    cosine = dot(both, full[0])
    sine = dot(both, full[1])
    cosine = cosine[:LANES] + (cosine[LANES:] + dot(both[:LANES], full[2]))
    sine = sine[:LANES] + (sine[LANES:] + dot(both[:LANES], full[3]))
    if sign < 0:
        return cosine[:HALF] + sine[HALF:], cosine[HALF:] - sine[:HALF]
    return cosine[:HALF] - sine[HALF:], cosine[HALF:] + sine[:HALF]


def to_tiles(real, imag, roll):
    parts = [x.reshape(LEVELS, 2, ROWS, N) for x in (real, imag)]
    rows = [parts[c][:, du] for c in range(2) for du in range(2)]
    halves = [block_swap([x[:, :, LANES * h : LANES * (h + 1)] for x in rows], roll) for h in range(2)]
    return jnp.stack([halves[h][b] for h in range(2) for b in range(4)])


def from_tiles(tiles, roll):
    halves = [block_swap([tiles[:, 4 * h + b] for b in range(4)], roll) for h in range(2)]
    rows = [jnp.concatenate([halves[0][b], halves[1][b]], axis=-1) for b in range(4)]
    return (
        jnp.stack([rows[0], rows[1]], axis=1).reshape(HALF, N),
        jnp.stack([rows[2], rows[3]], axis=1).reshape(HALF, N),
    )


def signs(shape):
    return jnp.where(lanes(shape) < HALF, 1.0, -1.0).astype(jnp.float32)


def along_x(x, full, sign, roll):
    high, low = split(x)
    wide = dot(full[0:2].reshape(2 * N, N), jnp.concatenate([high, low], axis=1))
    rest = dot(full[2:4].reshape(2 * N, N), high)
    total = wide[:, :LANES] + (wide[:, LANES:] + rest)
    return total[:N] + sign * roll(total[N:], HALF)


def turned(x, cosine, sine, roll):
    return x * cosine + roll(x, HALF) * sine


def middle(x, mult_real, mult_imag, full, roll):
    sign = signs((N, LANES))
    x = along_x(x, full, sign, roll)
    x = turned(x, mult_real, mult_imag, roll)
    return along_x(x, full, -sign, roll)


def is_down(shape):
    return (lanes(shape) // WAVES) % 2 == 0


def packed(even, odd, roll):
    down = is_down(even.shape)
    return jnp.where(down, even, roll(odd, WAVES)), jnp.where(down, roll(even, LANES - WAVES), odd)


def wrapped_numbers(index):
    folded = jnp.where(index < N // 2, index, index - N)
    return folded.astype(jnp.float32) * (2.0 * math.pi / N)


def multiplier(member, slow):
    row = lax.broadcasted_iota(jnp.int32, (N, LANES), 0)
    lane = lax.broadcasted_iota(jnp.int32, (N, LANES), 1)
    wave_x = wrapped_numbers(row)
    wave_y = wrapped_numbers(WAVES * member + lane % WAVES)
    argument = (OMEGA * slow) ** 2 - (wave_x * wave_x + wave_y * wave_y)
    vertical = jnp.sqrt(jnp.maximum(argument, 0.0))
    factor = jnp.exp(-jnp.sqrt(jnp.maximum(-argument, 0.0))) * (1.0 / (N * N))
    return factor * jnp.cos(vertical), signs((N, LANES)) * (factor * jnp.sin(vertical))


def mixed(real, imag, corr, refl, heads, tails, source):
    out = []
    for part in range(2):
        if part == 0:
            prop = real * corr[0] + imag * corr[1]
        else:
            prop = imag * corr[0] - real * corr[1]
        down = jnp.where(heads, source[part], prop[0])
        up = jnp.where(tails, 0.0, prop[1])
        out.append((down - refl * up, up + refl * down))
    return out


def kernel(
    down_real, down_imag, up_real, up_imag, slowness, ref_slow, reflect, source_real, source_imag,
    full_hbm, out_state,
    state, slow, source, full,
    mult, context, corr, sent_there, got_there, sent_back, got_back, got_last, tiles, edge_sent, edge_got,
    in_sems, out_sems, there_send, there_recv, back_send, back_recv, last_send, last_recv,
    edge_send, edge_recv, context_send, context_recv, source_send, source_recv,
):
    me = lax.axis_index("lat")
    depth = lax.axis_index("depth")
    depths = lax.axis_size("depth")
    cell_x, cell_y, core = me // 8, lax.rem(me // 2, 4), lax.rem(me, 2)
    member = 4 * lax.rem(cell_x, 2) + 2 * lax.rem(cell_y, 2) + core
    block = jnp.where(cell_x >= 2, 3 - cell_y // 2, cell_y // 2)
    flipped = lax.rem(depth, 2)
    level = jnp.where(flipped == 1, LEVELS - 1 - block, block)
    has_above = depth > 0
    has_below = depth < depths - 1
    last = TICKS - 1

    def block_of(z):
        return jnp.where(flipped == 1, LEVELS - 1 - z, z)

    def device_of(block, member):
        block_x, block_y = block // 2, lax.rem(block + 1, 4) // 2
        return 16 * block_x + 4 * block_y + 8 * (member // 4) + lax.rem(member, 4)

    def roll(x, shift):
        return pltpu.roll(x, shift, x.ndim - 1)

    def remote(src, dst, send_sem, recv_sem, where):
        return pltpu.make_async_remote_copy(
            src_ref=src, dst_ref=dst, send_sem=send_sem, recv_sem=recv_sem,
            device_id=where, device_id_type=MESH,
        )

    neighbour = (depth, lax.bitwise_xor(me, 1))

    loads = [
        pltpu.make_async_copy(src, dst, in_sems.at[n])
        for n, (src, dst) in enumerate([
            (down_real, state.at[0, :, 0]), (up_real, state.at[0, :, 1]),
            (down_imag, state.at[1, :, 0]), (up_imag, state.at[1, :, 1]),
            (full_hbm, full), (slowness, slow), (reflect, context.at[1, :, 2]),
            (source_real, source.at[0, 0]), (source_imag, source.at[0, 1]),
        ])
    ]
    for load in loads:
        load.start()

    barrier = pltpu.get_barrier_semaphore()

    def greet(step, _):
        pl.semaphore_signal(
            barrier, inc=1, device_id=(depth, lax.bitwise_xor(me, step)), device_id_type=MESH
        )
        return 0

    lax.fori_loop(1, LAT, greet, 0)

    @pl.when(has_above)
    def _():
        pl.semaphore_signal(barrier, inc=1, device_id=(depth - 1, me), device_id_type=MESH)

    @pl.when(has_below)
    def _():
        pl.semaphore_signal(barrier, inc=1, device_id=(depth + 1, me), device_id_type=MESH)

    for load in loads[:5]:
        load.wait()

    def first_there():
        pl.semaphore_wait(barrier, LAT - 1 + has_above.astype(jnp.int32) + has_below.astype(jnp.int32))

        def send(step, _):
            peer = lax.bitwise_xor(me, lax.bitwise_xor(step, FAR))
            peer_x, peer_y = peer // 8, lax.rem(peer // 2, 4)
            peer_block = jnp.where(peer_x >= 2, 3 - peer_y // 2, peer_y // 2)
            peer_member = 4 * lax.rem(peer_x, 2) + 2 * lax.rem(peer_y, 2) + lax.rem(peer, 2)
            remote(
                sent_there.at[0, peer_member, block_of(peer_block)],
                got_there.at[0, me], there_send.at[0], there_recv.at[0], (depth, peer),
            ).start()
            return 0

        lax.fori_loop(0, FAR, send, 0)
        lax.fori_loop(FAR + 1, LAT, send, 0)
        got_there[0, me] = sent_there[0, member, level]
        for load in loads[5:]:
            load.wait()
        for z in range(LEVELS):
            slow[z] = OMEGA * (slow[z] - ref_slow[z])
        edge_sent[0] = slow[LEVELS - 1]
        edge_sent[1] = slow[0]
        down = remote(edge_sent.at[0], edge_got.at[0], edge_send.at[0], edge_recv.at[0], (depth + 1, me))
        up = remote(edge_sent.at[1], edge_got.at[1], edge_send.at[1], edge_recv.at[1], (depth - 1, me))

        @pl.when(has_below)
        def _():
            down.start()

        @pl.when(has_above)
        def _():
            up.start()

        for z in range(LEVELS - 1):
            context[1, z + 1, 0] = slow[z]
            context[1, z, 1] = slow[z + 1]
        mine = ref_slow[0]
        for z in range(1, LEVELS):
            mine = jnp.where(level == z, ref_slow[z], mine)
        mult[0], mult[1] = multiplier(member, mine)
        nothing = jnp.zeros((ROWS, N), jnp.float32)

        @pl.when(has_above)
        def _():
            down.wait_recv()
            context[1, 0, 0] = edge_got[0]

        @pl.when(jnp.logical_not(has_above))
        def _():
            context[1, 0, 0] = nothing

        @pl.when(has_below)
        def _():
            up.wait_recv()
            context[1, LEVELS - 1, 1] = edge_got[1]

        @pl.when(jnp.logical_not(has_below))
        def _():
            context[1, LEVELS - 1, 1] = nothing

        holder = me // LEVELS
        place = lax.rem(me, LEVELS)
        for z in range(LEVELS):
            target = device_of(block_of(z), holder)

            @pl.when(target != me)
            def _():
                remote(
                    context.at[1, z], context.at[0, place], context_send, context_recv, (depth, target)
                ).start()

            @pl.when(target == me)
            def _():
                context[0, place] = context[1, z]

        @pl.when(jnp.logical_not(has_above))
        def _():
            target = device_of(0, holder)

            @pl.when(target != me)
            def _():
                remote(
                    source.at[0], source.at[1 + place], source_send, source_recv, (depth, target)
                ).start()

            @pl.when(target == me)
            def _():
                source[1 + place] = source[0]

    def later_there(tick):
        def send(step, _):
            peer = lax.bitwise_xor(member, GROUP - step)
            remote(
                sent_there.at[tick, peer], got_there.at[tick, pl.ds(LEVELS * member, LEVELS)],
                there_send.at[tick], there_recv.at[tick], (depth, device_of(block, peer)),
            ).start()
            return 0

        lax.fori_loop(1, GROUP, send, 0)
        got_there[tick, pl.ds(LEVELS * member, LEVELS)] = sent_there[tick, member]

    def far_member(to_block):
        across = (to_block // 2) != (block // 2)
        return jnp.where(to_block == block, 6, jnp.where(across, 2, 4))

    def group_back(tick):
        is_last = level == LEVELS - 1
        is_first = level == 0
        down_depth = depth + is_last.astype(jnp.int32)
        up_depth = depth - is_first.astype(jnp.int32)
        forth = jnp.where(flipped == 1, -1, 1)
        down_block = block + jnp.where(is_last, 0, forth)
        up_block = block - jnp.where(is_first, 0, forth)
        goes_down = jnp.logical_or(has_below, jnp.logical_not(is_last))
        goes_up = jnp.logical_or(has_above, jnp.logical_not(is_first))
        sides = (
            (0, goes_down, down_depth, down_block, far_member(down_block)),
            (1, goes_up, up_depth, up_block, far_member(up_block)),
        )

        def send(step, _):
            for side, goes, to_depth, to_block, far in sides:
                @pl.when(goes)
                def _():
                    peer = lax.bitwise_xor(member, lax.bitwise_xor(step, far))
                    remote(
                        sent_back.at[tick, pl.ds(LAT // 2 * side + 2 * peer, 2)],
                        got_back.at[tick, side, pl.ds(2 * member, 2)],
                        back_send.at[tick, side], back_recv.at[tick, side],
                        (to_depth, device_of(to_block, peer)),
                    ).start()

            return 0

        lax.fori_loop(0, GROUP, send, 0)
        return goes_down, goes_up

    def group_back_waits(tick, side):
        return remote(
            sent_back.at[tick, pl.ds(LAT // 2 * side, LAT // 2)], got_back.at[tick, side],
            back_send.at[tick, side], back_recv.at[tick, side], neighbour,
        )

    def last_waits(side, count, to):
        return remote(
            sent_back.at[last, pl.ds(0, count)], got_last.at[pl.ds(to, count)],
            last_send.at[side], last_recv.at[side], neighbour,
        )

    def one_tick(tick, _):
        real = state[0].reshape(HALF, N)
        imag = state[1].reshape(HALF, N)
        real, imag = along_y(real, imag, full, -1)
        sent_there[tick] = to_tiles(real, imag, roll)

        @pl.when(tick == 0)
        def _():
            first_there()
            remote(
                got_there.at[0, pl.ds(0, LAT - 1)], got_there.at[0, pl.ds(0, LAT - 1)],
                there_send.at[0], there_recv.at[0], neighbour,
            ).wait_recv()

        @pl.when(tick > 0)
        def _():
            later_there(tick)
            remote(
                got_there.at[tick, pl.ds(0, LAT - LEVELS)],
                got_there.at[tick, pl.ds(0, LAT - LEVELS)],
                there_send.at[tick], there_recv.at[tick], neighbour,
            ).wait_recv()

        x = got_there[tick].reshape(N, LANES)
        x = middle(x, mult[0], mult[1], full, roll).reshape(LAT, ROWS, LANES)

        @pl.when(tick < last)
        def _():
            pairs = x.reshape(LAT // 2, 2, ROWS, LANES)
            down, up = packed(pairs[:, 0], pairs[:, 1], roll)
            sent_back[tick, : LAT // 2] = down
            sent_back[tick, LAT // 2 :] = up
            goes = group_back(tick)

            def fill(which):
                angle = context[which, :, 0:2]
                corr[which, 0] = jnp.cos(angle)
                corr[which, 1] = jnp.sin(angle)

            @pl.when(tick == 0)
            def _():
                here = me // LEVELS == member
                for count in (LEVELS - 1, LEVELS):
                    @pl.when(here == (count < LEVELS))
                    def _():
                        remote(
                            context.at[1, pl.ds(0, count)], context.at[0, pl.ds(0, count)],
                            context_send, context_recv, neighbour,
                        ).wait_recv()

                    @pl.when(jnp.logical_and(jnp.logical_not(has_above), block == 0))
                    def _():
                        @pl.when(here == (count < LEVELS))
                        def _():
                            remote(
                                source.at[pl.ds(0, count)], source.at[pl.ds(1, count)],
                                source_send, source_recv, neighbour,
                            ).wait_recv()

                fill(0)

            @pl.when(tick == 1)
            def _():
                fill(1)

            comes_down = jnp.logical_or(has_above, level > 0)
            comes_up = jnp.logical_or(has_below, level < LEVELS - 1)
            for side, comes in ((0, comes_down), (1, comes_up)):
                @pl.when(comes)
                def _():
                    group_back_waits(tick, side).wait_recv()

                @pl.when(jnp.logical_not(comes))
                def _():
                    got_back[tick, side] = jnp.zeros((LAT // 2, ROWS, LANES), jnp.float32)

            down = got_back[tick, 0].reshape(GROUP, 2, ROWS, LANES)
            up = got_back[tick, 1].reshape(GROUP, 2, ROWS, LANES)
            for j in range(2):
                tiles[2 * j], tiles[2 * j + 1] = packed(down[:, j], up[:, j], roll)
            for side in range(2):
                @pl.when(goes[side])
                def _():
                    group_back_waits(tick, side).wait_send()

        @pl.when(tick == last)
        def _():
            sent_back[last] = x
            slot = level * GROUP + member

            def send(step, _):
                peer = lax.bitwise_xor(me, lax.bitwise_xor(step, FAR))
                remote(
                    sent_back.at[last, peer], got_last.at[slot],
                    last_send.at[0], last_recv.at[0], (depth, peer),
                ).start()
                return 0

            def send_past(side, where, place):
                def send(step, _):
                    peer = lax.bitwise_xor(me, lax.bitwise_xor(step, FAR))
                    remote(
                        sent_back.at[last, peer], got_last.at[place + member],
                        last_send.at[side], last_recv.at[side], (where, peer),
                    ).start()
                    return 0

                lax.fori_loop(0, LAT, send, 0)

            goes_down = jnp.logical_and(level == LEVELS - 1, has_below)
            goes_up = jnp.logical_and(level == 0, has_above)

            @pl.when(goes_down)
            def _():
                send_past(1, depth + 1, LAT)

            @pl.when(goes_up)
            def _():
                send_past(2, depth - 1, LAT + GROUP)

            lax.fori_loop(0, FAR, send, 0)
            lax.fori_loop(FAR + 1, LAT, send, 0)
            got_last[slot] = sent_back[last, me]
            for side, comes, place in ((1, has_above, LAT), (2, has_below, LAT + GROUP)):
                @pl.when(comes)
                def _():
                    last_waits(side, GROUP, place).wait_recv()

                @pl.when(jnp.logical_not(comes))
                def _():
                    got_last[pl.ds(place, GROUP)] = jnp.zeros((GROUP, ROWS, LANES), jnp.float32)

            last_waits(0, LAT - 1, 0).wait_recv()
            down = is_down((GROUP, ROWS, LANES))
            for z in range(LEVELS):
                above = GROUP * (z - 1) if z > 0 else LAT
                below = GROUP * (z + 1) if z < LEVELS - 1 else LAT + GROUP
                tiles[z] = jnp.where(
                    down, got_last[above : above + GROUP], got_last[below : below + GROUP]
                )
            last_waits(0, LAT - 1, 0).wait_send()
            for side, goes in ((1, goes_down), (2, goes_up)):
                @pl.when(goes)
                def _():
                    last_waits(side, LAT, 0).wait_send()

        real, imag = along_y(*from_tiles(tiles[...], roll), full, 1)
        real = real.reshape(LEVELS, 2, ROWS, N)
        imag = imag.reshape(LEVELS, 2, ROWS, N)
        at_end = (tick == last).astype(jnp.int32)
        for g in range(LEVELS):
            heads = jnp.logical_and(jnp.logical_not(has_above), jnp.where(tick == last, g, level) == 0)
            tails = jnp.logical_and(
                jnp.logical_not(has_below), jnp.where(tick == last, g, level) == LEVELS - 1
            )
            origin = source[jnp.where(tick == last, 0, 1 + g)]
            parts = mixed(
                real[g], imag[g], corr[at_end, :, g], context[at_end, g, 2], heads, tails, origin
            )
            for part in range(2):
                state[part, g, 0], state[part, g, 1] = parts[part]
        return 0

    lax.fori_loop(0, TICKS, one_tick, 0)
    store = pltpu.make_async_copy(state, out_state, out_sems.at[0])
    store.start()

    remote(
        got_there.at[0, pl.ds(0, LAT - 1)], got_there.at[0, pl.ds(0, LAT - 1)],
        there_send.at[0], there_recv.at[0], neighbour,
    ).wait_send()
    for tick in range(1, TICKS):
        remote(
            got_there.at[tick, pl.ds(0, LAT - LEVELS)], got_there.at[tick, pl.ds(0, LAT - LEVELS)],
            there_send.at[tick], there_recv.at[tick], neighbour,
        ).wait_send()
    holder = me // LEVELS
    here = holder == member
    for count in (LEVELS - 1, LEVELS):
        @pl.when(here == (count < LEVELS))
        def _():
            remote(
                context.at[1, pl.ds(0, count)], context.at[0, pl.ds(0, count)],
                context_send, context_recv, neighbour,
            ).wait_send()

    @pl.when(jnp.logical_and(jnp.logical_not(has_above), device_of(0, holder) != me))
    def _():
        remote(source.at[0], source.at[1], source_send, source_recv, neighbour).wait_send()

    for side, goes in ((0, has_below), (1, has_above)):
        @pl.when(goes)
        def _():
            remote(
                edge_sent.at[side], edge_got.at[side], edge_send.at[side], edge_recv.at[side], neighbour
            ).wait_send()

    store.wait()


def handed_out(state, out_dr, out_di, out_ur, out_ui):
    out_dr[...] = state[0, :, 0]
    out_di[...] = state[1, :, 0]
    out_ur[...] = state[0, :, 1]
    out_ui[...] = state[1, :, 1]


def solution(mesh):
    full = constants()
    plane = jax.ShapeDtypeStruct((LEVELS, ROWS, N), jnp.float32)
    anywhere = pl.BlockSpec(memory_space=pl.ANY)
    smem = pl.BlockSpec(memory_space=pltpu.SMEM)
    whole = pl.BlockSpec(memory_space=pltpu.VMEM)
    f32 = jnp.float32

    def step(*args):
        state = pl.pallas_call(
            kernel,
            out_shape=jax.ShapeDtypeStruct((2, LEVELS, 2, ROWS, N), f32),
            in_specs=[anywhere] * 5 + [smem] + [anywhere] * 4,
            out_specs=anywhere,
            scratch_shapes=[
                pltpu.VMEM((2, LEVELS, 2, ROWS, N), f32),
                pltpu.VMEM((LEVELS, ROWS, N), f32),
                pltpu.VMEM((1 + LEVELS, 2, ROWS, N), f32),
                pltpu.VMEM(full.shape, jnp.bfloat16),
                pltpu.VMEM((2, N, LANES), f32),
                pltpu.VMEM((2, LEVELS, 3, ROWS, N), f32),
                pltpu.VMEM((2, 2, LEVELS, 2, ROWS, N), f32),
                pltpu.VMEM((TICKS, GROUP, LEVELS, ROWS, LANES), f32),
                pltpu.VMEM((TICKS, LAT, ROWS, LANES), f32),
                pltpu.VMEM((TICKS, LAT, ROWS, LANES), f32),
                pltpu.VMEM((TICKS - 1, 2, LAT // 2, ROWS, LANES), f32),
                pltpu.VMEM((LAT + 2 * GROUP, ROWS, LANES), f32),
                pltpu.VMEM((LEVELS, GROUP, ROWS, LANES), f32),
                *[pltpu.VMEM((2, ROWS, N), f32)] * 2,
                pltpu.SemaphoreType.DMA((9,)),
                pltpu.SemaphoreType.DMA((1,)),
                *[pltpu.SemaphoreType.DMA((TICKS,))] * 2,
                *[pltpu.SemaphoreType.DMA((TICKS - 1, 2))] * 2,
                *[pltpu.SemaphoreType.DMA((3,))] * 2,
                *[pltpu.SemaphoreType.DMA((2,))] * 2,
                *[pltpu.SemaphoreType.DMA] * 4,
            ],
            compiler_params=pltpu.CompilerParams(collective_id=0, has_side_effects=True),
        )(*args, jnp.asarray(full))
        return pl.pallas_call(
            handed_out,
            out_shape=[plane] * 4,
            in_specs=[whole],
            out_specs=[whole] * 4,
        )(state)

    lateral = P("depth", "lat", None)
    return jax.shard_map(
        step,
        mesh=mesh,
        in_specs=(lateral,) * 5 + (P("depth"), lateral, P("lat", None), P("lat", None)),
        out_specs=(lateral,) * 4,
        check_vma=False,
    )
```

```python
import math

import jax
import jax.numpy as jnp
import ml_dtypes
import numpy as np
from jax import lax
from jax.experimental import pallas as pl
from jax.experimental.pallas import tpu as pltpu
from jax.sharding import PartitionSpec as P

TICKS = 3
OMEGA = 2.5
MESH = pl.DeviceIdType.MESH

LEVELS = 4
GROUP = 8
LAT = 32
FAR = 20
ROWS = 8
N = 256
LANES = 128
HALF = 64
WAVES = N // GROUP


def split(x):
    high = x.astype(jnp.bfloat16)
    low = (x - high.astype(jnp.float32)).astype(jnp.bfloat16)
    return high, low


def np_split(x):
    x = np.asarray(x, np.float64)
    high = x.astype(np.float32).astype(ml_dtypes.bfloat16)
    low = (x - high.astype(np.float64)).astype(np.float32).astype(ml_dtypes.bfloat16)
    return high, low


def constants():
    index = np.arange(N)
    angle = 2.0 * np.pi * (np.outer(index, index) % N) / N
    cos_hi, cos_lo = np_split(np.cos(angle))
    sin_hi, sin_lo = np_split(np.sin(angle))
    return np.stack([cos_hi, sin_hi, cos_lo, sin_lo])


def dot(a, b, dims=((1,), (0,))):
    return lax.dot_general(a, b, (dims, ((), ())), preferred_element_type=jnp.float32)


def lanes(shape):
    return lax.broadcasted_iota(jnp.int32, shape, len(shape) - 1)


def block_swap(tiles, roll):
    block = lanes(tiles[0].shape) // WAVES
    for bit in (2, 1):
        keep = (block & bit) == 0
        shift = bit * WAVES
        new = list(tiles)
        for a in range(4):
            if a & bit == 0:
                low, high = tiles[a], tiles[a + bit]
                new[a] = jnp.where(keep, low, roll(high, shift))
                new[a + bit] = jnp.where(keep, roll(low, LANES - shift), high)
        tiles = new
    return tiles


def along_y(real, imag, full, sign):
    real_hi, real_lo = split(real)
    imag_hi, imag_lo = split(imag)
    both = jnp.concatenate([real_hi, imag_hi, real_lo, imag_lo], axis=0)
    cosine = dot(both, full[0])
    sine = dot(both, full[1])
    cosine = cosine[:LANES] + (cosine[LANES:] + dot(both[:LANES], full[2]))
    sine = sine[:LANES] + (sine[LANES:] + dot(both[:LANES], full[3]))
    if sign < 0:
        return cosine[:HALF] + sine[HALF:], cosine[HALF:] - sine[:HALF]
    return cosine[:HALF] - sine[HALF:], cosine[HALF:] + sine[:HALF]


def to_tiles(real, imag, roll):
    parts = [x.reshape(LEVELS, 2, ROWS, N) for x in (real, imag)]
    rows = [parts[c][:, du] for c in range(2) for du in range(2)]
    halves = [block_swap([x[:, :, LANES * h : LANES * (h + 1)] for x in rows], roll) for h in range(2)]
    return jnp.stack([halves[h][b] for h in range(2) for b in range(4)])


def from_tiles(x, roll):
    halves = [block_swap([x[4 * h + a] for a in range(4)], roll) for h in range(2)]
    return [jnp.concatenate([halves[0][b], halves[1][b]], axis=-1) for b in range(4)]


def from_pairs(x, roll):
    rows = [from_tiles(x[:, j], roll) for j in range(2)]
    return [jnp.stack([rows[g // 2][2 * part + g % 2] for g in range(LEVELS)]) for part in range(2)]


def signs(shape):
    return jnp.where(lanes(shape) < HALF, 1.0, -1.0).astype(jnp.float32)


def along_x(x, full, sign, roll):
    high, low = split(x)
    wide = dot(full[0:2].reshape(2 * N, N), jnp.concatenate([high, low], axis=1))
    rest = dot(full[2:4].reshape(2 * N, N), high)
    total = wide[:, :LANES] + (wide[:, LANES:] + rest)
    return total[:N] + sign * roll(total[N:], HALF)


def turned(x, cosine, sine, roll):
    return x * cosine + roll(x, HALF) * sine


def middle(x, mult_real, mult_imag, full, roll):
    sign = signs((N, LANES))
    x = along_x(x, full, sign, roll)
    x = turned(x, mult_real, mult_imag, roll)
    return along_x(x, full, -sign, roll)


def is_down(shape):
    return (lanes(shape) // WAVES) % 2 == 0


def packed(even, odd, roll):
    down = is_down(even.shape)
    return jnp.where(down, even, roll(odd, WAVES)), jnp.where(down, roll(even, LANES - WAVES), odd)


def wrapped_numbers(index):
    folded = jnp.where(index < N // 2, index, index - N)
    return folded.astype(jnp.float32) * (2.0 * math.pi / N)


def multiplier(member, slow):
    row = lax.broadcasted_iota(jnp.int32, (N, LANES), 0)
    lane = lax.broadcasted_iota(jnp.int32, (N, LANES), 1)
    wave_x = wrapped_numbers(row)
    wave_y = wrapped_numbers(WAVES * member + lane % WAVES)
    argument = (OMEGA * slow) ** 2 - (wave_x * wave_x + wave_y * wave_y)
    vertical = jnp.sqrt(jnp.maximum(argument, 0.0))
    factor = jnp.exp(-jnp.sqrt(jnp.maximum(-argument, 0.0))) * (1.0 / (N * N))
    return factor * jnp.cos(vertical), signs((N, LANES)) * (factor * jnp.sin(vertical))


def mixed(real, imag, corr, refl, heads, tails, source):
    out = []
    for part in range(2):
        if part == 0:
            prop = real * corr[0] + imag * corr[1]
        else:
            prop = imag * corr[0] - real * corr[1]
        down = jnp.where(heads, source[part], prop[0])
        up = jnp.where(tails, 0.0, prop[1])
        out.append((down - refl * up, up + refl * down))
    return out


def kernel(
    down_real, down_imag, up_real, up_imag, slowness, ref_slow, reflect, source_real, source_imag,
    full_hbm, state,
    slow, source, full,
    mult, context, corr, sent_there, got_there, sent_back, got_back, got_last, edge_sent, edge_got,
    in_sems, there_send, there_recv, back_send, back_recv, last_send, last_recv,
    edge_send, edge_recv, context_send, context_recv, source_send, source_recv,
):
    me = lax.axis_index("lat")
    depth = lax.axis_index("depth")
    depths = lax.axis_size("depth")
    cell_x, cell_y, core = me // 8, lax.rem(me // 2, 4), lax.rem(me, 2)
    member = 4 * lax.rem(cell_x, 2) + 2 * lax.rem(cell_y, 2) + core
    block = jnp.where(cell_x >= 2, 3 - cell_y // 2, cell_y // 2)
    flipped = lax.rem(depth, 2)
    level = jnp.where(flipped == 1, LEVELS - 1 - block, block)
    has_above = depth > 0
    has_below = depth < depths - 1
    last = TICKS - 1

    def block_of(z):
        return jnp.where(flipped == 1, LEVELS - 1 - z, z)

    def device_of(block, member):
        block_x, block_y = block // 2, lax.rem(block + 1, 4) // 2
        return 16 * block_x + 4 * block_y + 8 * (member // 4) + lax.rem(member, 4)

    def roll(x, shift):
        return pltpu.roll(x, shift, x.ndim - 1)

    def remote(src, dst, send_sem, recv_sem, where):
        return pltpu.make_async_remote_copy(
            src_ref=src, dst_ref=dst, send_sem=send_sem, recv_sem=recv_sem,
            device_id=where, device_id_type=MESH,
        )

    neighbour = (depth, lax.bitwise_xor(me, 1))

    loads = [
        pltpu.make_async_copy(src, dst, in_sems.at[n])
        for n, (src, dst) in enumerate([
            (down_real, state.at[0, :, 0]), (up_real, state.at[0, :, 1]),
            (down_imag, state.at[1, :, 0]), (up_imag, state.at[1, :, 1]),
            (full_hbm, full), (slowness, slow), (reflect, context.at[1, :, 2]),
            (source_real, source.at[0, 0]), (source_imag, source.at[0, 1]),
        ])
    ]
    for load in loads:
        load.start()

    barrier = pltpu.get_barrier_semaphore()

    def greet(step, _):
        peer = lax.bitwise_xor(me, lax.bitwise_xor(step, FAR))
        pl.semaphore_signal(barrier, inc=1, device_id=(depth, peer), device_id_type=MESH)
        return 0

    lax.fori_loop(0, FAR, greet, 0)
    lax.fori_loop(FAR + 1, LAT, greet, 0)

    @pl.when(has_above)
    def _():
        pl.semaphore_signal(barrier, inc=1, device_id=(depth - 1, me), device_id_type=MESH)

    @pl.when(has_below)
    def _():
        pl.semaphore_signal(barrier, inc=1, device_id=(depth + 1, me), device_id_type=MESH)

    for load in loads[:5]:
        load.wait()

    def first_there():
        pl.semaphore_wait(barrier, LAT - 1 + has_above.astype(jnp.int32) + has_below.astype(jnp.int32))

        def send(step, _):
            peer = lax.bitwise_xor(me, lax.bitwise_xor(step, FAR))
            peer_x, peer_y = peer // 8, lax.rem(peer // 2, 4)
            peer_block = jnp.where(peer_x >= 2, 3 - peer_y // 2, peer_y // 2)
            peer_member = 4 * lax.rem(peer_x, 2) + 2 * lax.rem(peer_y, 2) + lax.rem(peer, 2)
            remote(
                sent_there.at[0, peer_member, block_of(peer_block)],
                got_there.at[0, me], there_send.at[0], there_recv.at[0], (depth, peer),
            ).start()
            return 0

        lax.fori_loop(0, FAR, send, 0)
        lax.fori_loop(FAR + 1, LAT, send, 0)
        got_there[0, me] = sent_there[0, member, level]
        for load in loads[5:]:
            load.wait()
        for z in range(LEVELS):
            slow[z] = OMEGA * (slow[z] - ref_slow[z])
        edge_sent[0] = slow[LEVELS - 1]
        edge_sent[1] = slow[0]
        down = remote(edge_sent.at[0], edge_got.at[0], edge_send.at[0], edge_recv.at[0], (depth + 1, me))
        up = remote(edge_sent.at[1], edge_got.at[1], edge_send.at[1], edge_recv.at[1], (depth - 1, me))

        @pl.when(has_below)
        def _():
            down.start()

        @pl.when(has_above)
        def _():
            up.start()

        for z in range(LEVELS - 1):
            context[1, z + 1, 0] = slow[z]
            context[1, z, 1] = slow[z + 1]
        mine = ref_slow[0]
        for z in range(1, LEVELS):
            mine = jnp.where(level == z, ref_slow[z], mine)
        mult[0], mult[1] = multiplier(member, mine)
        nothing = jnp.zeros((ROWS, N), jnp.float32)

        @pl.when(has_above)
        def _():
            down.wait_recv()
            context[1, 0, 0] = edge_got[0]

        @pl.when(jnp.logical_not(has_above))
        def _():
            context[1, 0, 0] = nothing

        @pl.when(has_below)
        def _():
            up.wait_recv()
            context[1, LEVELS - 1, 1] = edge_got[1]

        @pl.when(jnp.logical_not(has_below))
        def _():
            context[1, LEVELS - 1, 1] = nothing

        holder = me // LEVELS
        place = lax.rem(me, LEVELS)
        for z in range(LEVELS):
            target = device_of(block_of(z), holder)

            @pl.when(target != me)
            def _():
                remote(
                    context.at[1, z], context.at[0, place], context_send, context_recv, (depth, target)
                ).start()

            @pl.when(target == me)
            def _():
                context[0, place] = context[1, z]

        @pl.when(jnp.logical_not(has_above))
        def _():
            target = device_of(0, holder)

            @pl.when(target != me)
            def _():
                remote(
                    source.at[0], source.at[1 + place], source_send, source_recv, (depth, target)
                ).start()

            @pl.when(target == me)
            def _():
                source[1 + place] = source[0]

    def later_there(tick):
        def send(step, _):
            peer = lax.bitwise_xor(member, GROUP - step)
            remote(
                sent_there.at[tick, peer], got_there.at[tick, pl.ds(LEVELS * member, LEVELS)],
                there_send.at[tick], there_recv.at[tick], (depth, device_of(block, peer)),
            ).start()
            return 0

        lax.fori_loop(1, GROUP, send, 0)
        got_there[tick, pl.ds(LEVELS * member, LEVELS)] = sent_there[tick, member]

    def far_member(to_block):
        across = (to_block // 2) != (block // 2)
        return jnp.where(to_block == block, 6, jnp.where(across, 2, 4))

    def group_back(tick):
        is_last = level == LEVELS - 1
        is_first = level == 0
        down_depth = depth + is_last.astype(jnp.int32)
        up_depth = depth - is_first.astype(jnp.int32)
        forth = jnp.where(flipped == 1, -1, 1)
        down_block = block + jnp.where(is_last, 0, forth)
        up_block = block - jnp.where(is_first, 0, forth)
        goes_down = jnp.logical_or(has_below, jnp.logical_not(is_last))
        goes_up = jnp.logical_or(has_above, jnp.logical_not(is_first))
        sides = (
            (0, goes_down, down_depth, down_block, far_member(down_block)),
            (1, goes_up, up_depth, up_block, far_member(up_block)),
        )

        def send(step, _):
            for side, goes, to_depth, to_block, far in sides:
                @pl.when(goes)
                def _():
                    peer = lax.bitwise_xor(member, lax.bitwise_xor(step, far))
                    remote(
                        sent_back.at[tick, pl.ds(LAT // 2 * side + 2 * peer, 2)],
                        got_back.at[tick, side, pl.ds(2 * member, 2)],
                        back_send.at[tick, side], back_recv.at[tick, side],
                        (to_depth, device_of(to_block, peer)),
                    ).start()

            return 0

        lax.fori_loop(0, GROUP, send, 0)
        return goes_down, goes_up

    def group_back_waits(tick, side):
        return remote(
            sent_back.at[tick, pl.ds(LAT // 2 * side, LAT // 2)], got_back.at[tick, side],
            back_send.at[tick, side], back_recv.at[tick, side], neighbour,
        )

    def last_waits(side, count, to):
        return remote(
            sent_back.at[last, pl.ds(0, count)], got_last.at[pl.ds(to, count)],
            last_send.at[side], last_recv.at[side], neighbour,
        )

    def one_tick(tick, _):
        real = state[0].reshape(HALF, N)
        imag = state[1].reshape(HALF, N)
        real, imag = along_y(real, imag, full, -1)
        sent_there[tick] = to_tiles(real, imag, roll)

        @pl.when(tick == 0)
        def _():
            first_there()
            remote(
                got_there.at[0, pl.ds(0, LAT - 1)], got_there.at[0, pl.ds(0, LAT - 1)],
                there_send.at[0], there_recv.at[0], neighbour,
            ).wait_recv()

        @pl.when(tick > 0)
        def _():
            later_there(tick)
            remote(
                got_there.at[tick, pl.ds(0, LAT - LEVELS)],
                got_there.at[tick, pl.ds(0, LAT - LEVELS)],
                there_send.at[tick], there_recv.at[tick], neighbour,
            ).wait_recv()

        x = got_there[tick].reshape(N, LANES)
        x = middle(x, mult[0], mult[1], full, roll).reshape(LAT, ROWS, LANES)

        @pl.when(tick < last)
        def _():
            pairs = x.reshape(LAT // 2, 2, ROWS, LANES)
            down, up = packed(pairs[:, 0], pairs[:, 1], roll)
            sent_back[tick, : LAT // 2] = down
            sent_back[tick, LAT // 2 :] = up
            goes = group_back(tick)

            def fill(which):
                angle = context[which, :, 0:2]
                corr[which, 0] = jnp.cos(angle)
                corr[which, 1] = jnp.sin(angle)

            @pl.when(tick == 0)
            def _():
                here = me // LEVELS == member
                for count in (LEVELS - 1, LEVELS):
                    @pl.when(here == (count < LEVELS))
                    def _():
                        remote(
                            context.at[1, pl.ds(0, count)], context.at[0, pl.ds(0, count)],
                            context_send, context_recv, neighbour,
                        ).wait_recv()

                    @pl.when(jnp.logical_and(jnp.logical_not(has_above), block == 0))
                    def _():
                        @pl.when(here == (count < LEVELS))
                        def _():
                            remote(
                                source.at[pl.ds(0, count)], source.at[pl.ds(1, count)],
                                source_send, source_recv, neighbour,
                            ).wait_recv()

                fill(0)

            @pl.when(tick == 1)
            def _():
                fill(1)

            comes_down = jnp.logical_or(has_above, level > 0)
            comes_up = jnp.logical_or(has_below, level < LEVELS - 1)
            for side, comes in ((0, comes_down), (1, comes_up)):
                @pl.when(comes)
                def _():
                    group_back_waits(tick, side).wait_recv()

                @pl.when(jnp.logical_not(comes))
                def _():
                    got_back[tick, side] = jnp.zeros((LAT // 2, ROWS, LANES), jnp.float32)

            down = got_back[tick, 0].reshape(GROUP, 2, ROWS, LANES)
            up = got_back[tick, 1].reshape(GROUP, 2, ROWS, LANES)
            for du, got in enumerate((down, up)):
                for part, rows in enumerate(from_pairs(got, roll)):
                    state[part, :, du] = rows
            for side in range(2):
                @pl.when(goes[side])
                def _():
                    group_back_waits(tick, side).wait_send()

        @pl.when(tick == last)
        def _():
            sent_back[last] = x
            slot = level * GROUP + member

            goes_down = jnp.logical_and(level == LEVELS - 1, has_below)
            goes_up = jnp.logical_and(level == 0, has_above)

            def send(step, _):
                peer = lax.bitwise_xor(me, lax.bitwise_xor(step, FAR))

                def push(side, where, place):
                    remote(
                        sent_back.at[last, peer], got_last.at[place],
                        last_send.at[side], last_recv.at[side], (where, peer),
                    ).start()

                @pl.when(goes_down)
                def _():
                    push(1, depth + 1, LAT + member)

                @pl.when(goes_up)
                def _():
                    push(2, depth - 1, LAT + GROUP + member)

                @pl.when(peer != me)
                def _():
                    push(0, depth, slot)

                return 0

            lax.fori_loop(0, LAT, send, 0)
            got_last[slot] = sent_back[last, me]
            for side, comes, place in ((1, has_above, LAT), (2, has_below, LAT + GROUP)):
                @pl.when(comes)
                def _():
                    last_waits(side, GROUP, place).wait_recv()

                @pl.when(jnp.logical_not(comes))
                def _():
                    got_last[pl.ds(place, GROUP)] = jnp.zeros((GROUP, ROWS, LANES), jnp.float32)

            last_waits(0, LAT - 1, 0).wait_recv()
            down = is_down((GROUP, ROWS, LANES))
            for z in range(LEVELS):
                above = GROUP * (z - 1) if z > 0 else LAT
                below = GROUP * (z + 1) if z < LEVELS - 1 else LAT + GROUP
                got = jnp.where(down, got_last[above : above + GROUP], got_last[below : below + GROUP])
                for n, rows in enumerate(from_tiles(got, roll)):
                    state[n // 2, z, n % 2] = rows
            last_waits(0, LAT - 1, 0).wait_send()
            for side, goes in ((1, goes_down), (2, goes_up)):
                @pl.when(goes)
                def _():
                    last_waits(side, LAT, 0).wait_send()

        real, imag = along_y(state[0].reshape(HALF, N), state[1].reshape(HALF, N), full, 1)
        real = real.reshape(LEVELS, 2, ROWS, N)
        imag = imag.reshape(LEVELS, 2, ROWS, N)
        at_end = (tick == last).astype(jnp.int32)
        for g in range(LEVELS):
            heads = jnp.logical_and(jnp.logical_not(has_above), jnp.where(tick == last, g, level) == 0)
            tails = jnp.logical_and(
                jnp.logical_not(has_below), jnp.where(tick == last, g, level) == LEVELS - 1
            )
            origin = source[jnp.where(tick == last, 0, 1 + g)]
            parts = mixed(
                real[g], imag[g], corr[at_end, :, g], context[at_end, g, 2], heads, tails, origin
            )
            for part in range(2):
                state[part, g, 0], state[part, g, 1] = parts[part]
        return 0

    lax.fori_loop(0, TICKS, one_tick, 0)
    remote(
        got_there.at[0, pl.ds(0, LAT - 1)], got_there.at[0, pl.ds(0, LAT - 1)],
        there_send.at[0], there_recv.at[0], neighbour,
    ).wait_send()
    for tick in range(1, TICKS):
        remote(
            got_there.at[tick, pl.ds(0, LAT - LEVELS)], got_there.at[tick, pl.ds(0, LAT - LEVELS)],
            there_send.at[tick], there_recv.at[tick], neighbour,
        ).wait_send()
    holder = me // LEVELS
    here = holder == member
    for count in (LEVELS - 1, LEVELS):
        @pl.when(here == (count < LEVELS))
        def _():
            remote(
                context.at[1, pl.ds(0, count)], context.at[0, pl.ds(0, count)],
                context_send, context_recv, neighbour,
            ).wait_send()

    @pl.when(jnp.logical_and(jnp.logical_not(has_above), device_of(0, holder) != me))
    def _():
        remote(source.at[0], source.at[1], source_send, source_recv, neighbour).wait_send()

    for side, goes in ((0, has_below), (1, has_above)):
        @pl.when(goes)
        def _():
            remote(
                edge_sent.at[side], edge_got.at[side], edge_send.at[side], edge_recv.at[side], neighbour
            ).wait_send()


def handed_out(state, out_dr, out_di, out_ur, out_ui, sems):
    copies = [
        pltpu.make_async_copy(state.at[n % 2, :, n // 2], out, sems.at[n])
        for n, out in enumerate((out_dr, out_di, out_ur, out_ui))
    ]
    for copy in copies:
        copy.start()
    for copy in copies:
        copy.wait()


def solution(mesh):
    full = constants()
    plane = jax.ShapeDtypeStruct((LEVELS, ROWS, N), jnp.float32)
    anywhere = pl.BlockSpec(memory_space=pl.ANY)
    smem = pl.BlockSpec(memory_space=pltpu.SMEM)
    whole = pl.BlockSpec(memory_space=pltpu.VMEM)
    f32 = jnp.float32

    def step(*args):
        state = pl.pallas_call(
            kernel,
            out_shape=pltpu.VMEM((2, LEVELS, 2, ROWS, N), f32),
            in_specs=[anywhere] * 5 + [smem] + [anywhere] * 4,
            out_specs=whole,
            scratch_shapes=[
                pltpu.VMEM((LEVELS, ROWS, N), f32),
                pltpu.VMEM((1 + LEVELS, 2, ROWS, N), f32),
                pltpu.VMEM(full.shape, jnp.bfloat16),
                pltpu.VMEM((2, N, LANES), f32),
                pltpu.VMEM((2, LEVELS, 3, ROWS, N), f32),
                pltpu.VMEM((2, 2, LEVELS, 2, ROWS, N), f32),
                pltpu.VMEM((TICKS, GROUP, LEVELS, ROWS, LANES), f32),
                pltpu.VMEM((TICKS, LAT, ROWS, LANES), f32),
                pltpu.VMEM((TICKS, LAT, ROWS, LANES), f32),
                pltpu.VMEM((TICKS - 1, 2, LAT // 2, ROWS, LANES), f32),
                pltpu.VMEM((LAT + 2 * GROUP, ROWS, LANES), f32),
                *[pltpu.VMEM((2, ROWS, N), f32)] * 2,
                pltpu.SemaphoreType.DMA((9,)),
                *[pltpu.SemaphoreType.DMA((TICKS,))] * 2,
                *[pltpu.SemaphoreType.DMA((TICKS - 1, 2))] * 2,
                *[pltpu.SemaphoreType.DMA((3,))] * 2,
                *[pltpu.SemaphoreType.DMA((2,))] * 2,
                *[pltpu.SemaphoreType.DMA] * 4,
            ],
            compiler_params=pltpu.CompilerParams(collective_id=0, has_side_effects=True),
        )(*args, jnp.asarray(full))
        return pl.pallas_call(
            handed_out,
            out_shape=[plane] * 4,
            in_specs=[whole],
            out_specs=[anywhere] * 4,
            scratch_shapes=[pltpu.SemaphoreType.DMA((4,))],
            compiler_params=pltpu.CompilerParams(vmem_limit_bytes=2**20),
        )(state)

    lateral = P("depth", "lat", None)
    return jax.shard_map(
        step,
        mesh=mesh,
        in_specs=(lateral,) * 5 + (P("depth"), lateral, P("lat", None), P("lat", None)),
        out_specs=(lateral,) * 4,
        check_vma=False,
    )
```

```python
import math

import jax
import jax.numpy as jnp
import ml_dtypes
import numpy as np
from jax import lax
from jax.experimental import pallas as pl
from jax.experimental.pallas import tpu as pltpu
from jax.sharding import PartitionSpec as P

TICKS = 3
OMEGA = 2.5
MESH = pl.DeviceIdType.MESH

LEVELS = 4
GROUP = 8
LAT = 32
FAR = 20
ROWS = 8
N = 256
LANES = 128
HALF = 64
HALVES = N // 2
WAVES = N // GROUP


def split(x):
    high = x.astype(jnp.bfloat16)
    low = (x - high.astype(jnp.float32)).astype(jnp.bfloat16)
    return high, low


def np_split(x):
    x = np.asarray(x, np.float64)
    high = x.astype(np.float32).astype(ml_dtypes.bfloat16)
    low = (x - high.astype(np.float64)).astype(np.float32).astype(ml_dtypes.bfloat16)
    return high, low


def constants():
    index = np.arange(HALVES)
    angles = (
        2.0 * np.pi * (np.outer(2 * index, index) % N) / N,
        2.0 * np.pi * (np.outer(2 * index + 1, index) % N) / N,
    )
    even, odd = angles
    by_row = []
    for angle in (even, odd.T, odd):
        for part in np_split(np.concatenate([np.cos(angle), np.sin(angle)], axis=1)):
            by_row.append(np.concatenate([part, part], axis=0))
    by_column = []
    for angle in (even, odd, odd.T):
        by_column.extend(np_split(np.concatenate([np.cos(angle), np.sin(angle)], axis=0)))
    return np.stack(by_row), np.stack(by_column)


def dot(a, b, dims=((1,), (0,))):
    return lax.dot_general(a, b, (dims, ((), ())), preferred_element_type=jnp.float32)


def lanes(shape):
    return lax.broadcasted_iota(jnp.int32, shape, len(shape) - 1)


def block_swap(tiles, roll):
    block = lanes(tiles[0].shape) // WAVES
    for bit in (2, 1):
        keep = (block & bit) == 0
        shift = bit * WAVES
        new = list(tiles)
        for a in range(4):
            if a & bit == 0:
                low, high = tiles[a], tiles[a + bit]
                new[a] = jnp.where(keep, low, roll(high, shift))
                new[a + bit] = jnp.where(keep, roll(low, LANES - shift), high)
        tiles = new
    return tiles


def along_y(real, imag, rows, sign):
    x = jnp.concatenate([real, imag], axis=0)
    first, second = x[:, :HALVES], x[:, HALVES:]
    if sign < 0:
        first, second = first + second, first - second
    out = []
    for table, part in ((0, first), (2 if sign < 0 else 4, second)):
        both = jnp.concatenate(split(part), axis=1)
        total = dot(both, rows[table]) + dot(both, rows[table + 1])
        cosine, sine = total[:, :HALVES], total[:, HALVES:]
        if sign < 0:
            out.append((cosine[:HALF] + sine[HALF:], cosine[HALF:] - sine[:HALF]))
        else:
            out.append((cosine[:HALF] - sine[HALF:], cosine[HALF:] + sine[:HALF]))
    parts = []
    for first, second in zip(*out):
        if sign > 0:
            first, second = first + second, first - second
        parts.append(jnp.concatenate([first, second], axis=1))
    return parts


def to_tiles(real, imag, roll):
    parts = [x.reshape(LEVELS, 2, ROWS, N) for x in (real, imag)]
    rows = [parts[c][:, du] for c in range(2) for du in range(2)]
    halves = [block_swap([x[:, :, LANES * h : LANES * (h + 1)] for x in rows], roll) for h in range(2)]
    return jnp.stack([halves[h][b] for h in range(2) for b in range(4)])


def from_tiles(x, roll):
    halves = [block_swap([x[4 * h + a] for a in range(4)], roll) for h in range(2)]
    return [jnp.concatenate([halves[0][b], halves[1][b]], axis=-1) for b in range(4)]


def from_pairs(x, roll):
    rows = [from_tiles(x[:, j], roll) for j in range(2)]
    return [jnp.stack([rows[g // 2][2 * part + g % 2] for g in range(LEVELS)]) for part in range(2)]


def signs(shape):
    return jnp.where(lanes(shape) < HALF, 1.0, -1.0).astype(jnp.float32)


def along_x(x, columns, sign, roll):
    first, second = x[:HALVES], x[HALVES:]
    if sign < 0:
        first, second = first + second, first - second
    turn = -sign * signs((HALVES, LANES))
    out = []
    for table, part in ((0, first), (2 if sign < 0 else 4, second)):
        high, low = split(part)
        wide = dot(columns[table], jnp.concatenate([high, low], axis=1))
        total = wide[:, :LANES] + (wide[:, LANES:] + dot(columns[table + 1], high))
        out.append(total[:HALVES] + turn * roll(total[HALVES:], HALF))
    first, second = out
    if sign > 0:
        first, second = first + second, first - second
    return jnp.concatenate([first, second], axis=0)


def turned(x, cosine, sine, roll):
    return x * cosine + roll(x, HALF) * sine


def middle(x, mult_real, mult_imag, columns, roll):
    x = along_x(x, columns, -1, roll)
    x = turned(x, mult_real, mult_imag, roll)
    return along_x(x, columns, 1, roll)


def is_down(shape):
    return (lanes(shape) // WAVES) % 2 == 0


def packed(even, odd, roll):
    down = is_down(even.shape)
    return jnp.where(down, even, roll(odd, WAVES)), jnp.where(down, roll(even, LANES - WAVES), odd)


def wrapped_numbers(index):
    folded = jnp.where(index < N // 2, index, index - N)
    return folded.astype(jnp.float32) * (2.0 * math.pi / N)


def in_order(place):
    return jnp.where(place < HALVES, 2 * place, 2 * (place - HALVES) + 1)


def multiplier(member, slow):
    row = lax.broadcasted_iota(jnp.int32, (N, LANES), 0)
    lane = lax.broadcasted_iota(jnp.int32, (N, LANES), 1)
    wave_x = wrapped_numbers(in_order(row))
    wave_y = wrapped_numbers(in_order(WAVES * member + lane % WAVES))
    argument = (OMEGA * slow) ** 2 - (wave_x * wave_x + wave_y * wave_y)
    vertical = jnp.sqrt(jnp.maximum(argument, 0.0))
    factor = jnp.exp(-jnp.sqrt(jnp.maximum(-argument, 0.0))) * (1.0 / (N * N))
    return factor * jnp.cos(vertical), signs((N, LANES)) * (factor * jnp.sin(vertical))


def mixed(real, imag, corr, refl, heads, tails, source):
    out = []
    for part in range(2):
        if part == 0:
            prop = real * corr[0] + imag * corr[1]
        else:
            prop = imag * corr[0] - real * corr[1]
        down = jnp.where(heads, source[part], prop[0])
        up = jnp.where(tails, 0.0, prop[1])
        out.append((down - refl * up, up + refl * down))
    return out


def kernel(
    down_real, down_imag, up_real, up_imag, slowness, ref_slow, reflect, source_real, source_imag,
    rows_hbm, columns_hbm, state,
    slow, source, rows, columns,
    mult, context, corr, sent_there, got_there, sent_back, got_back, got_last, edge_sent, edge_got,
    in_sems, there_send, there_recv, back_send, back_recv, last_send, last_recv,
    edge_send, edge_recv, context_send, context_recv, source_send, source_recv,
):
    me = lax.axis_index("lat")
    depth = lax.axis_index("depth")
    depths = lax.axis_size("depth")
    cell_x, cell_y, core = me // 8, lax.rem(me // 2, 4), lax.rem(me, 2)
    member = 4 * lax.rem(cell_x, 2) + 2 * lax.rem(cell_y, 2) + core
    block = jnp.where(cell_x >= 2, 3 - cell_y // 2, cell_y // 2)
    flipped = lax.rem(depth, 2)
    level = jnp.where(flipped == 1, LEVELS - 1 - block, block)
    has_above = depth > 0
    has_below = depth < depths - 1
    last = TICKS - 1

    def block_of(z):
        return jnp.where(flipped == 1, LEVELS - 1 - z, z)

    def device_of(block, member):
        block_x, block_y = block // 2, lax.rem(block + 1, 4) // 2
        return 16 * block_x + 4 * block_y + 8 * (member // 4) + lax.rem(member, 4)

    def roll(x, shift):
        return pltpu.roll(x, shift, x.ndim - 1)

    def remote(src, dst, send_sem, recv_sem, where):
        return pltpu.make_async_remote_copy(
            src_ref=src, dst_ref=dst, send_sem=send_sem, recv_sem=recv_sem,
            device_id=where, device_id_type=MESH,
        )

    neighbour = (depth, lax.bitwise_xor(me, 1))

    loads = [
        pltpu.make_async_copy(src, dst, in_sems.at[n])
        for n, (src, dst) in enumerate([
            (down_real, state.at[0, :, 0]), (up_real, state.at[0, :, 1]),
            (down_imag, state.at[1, :, 0]), (up_imag, state.at[1, :, 1]),
            (rows_hbm, rows), (slowness, slow), (reflect, context.at[1, :, 2]),
            (source_real, source.at[0, 0]), (source_imag, source.at[0, 1]),
            (columns_hbm, columns),
        ])
    ]
    for load in loads:
        load.start()

    barrier = pltpu.get_barrier_semaphore()

    def greet(step, _):
        peer = lax.bitwise_xor(me, lax.bitwise_xor(step, FAR))
        pl.semaphore_signal(barrier, inc=1, device_id=(depth, peer), device_id_type=MESH)
        return 0

    lax.fori_loop(0, FAR, greet, 0)
    lax.fori_loop(FAR + 1, LAT, greet, 0)

    @pl.when(has_above)
    def _():
        pl.semaphore_signal(barrier, inc=1, device_id=(depth - 1, me), device_id_type=MESH)

    @pl.when(has_below)
    def _():
        pl.semaphore_signal(barrier, inc=1, device_id=(depth + 1, me), device_id_type=MESH)

    for load in loads[:5]:
        load.wait()

    def first_there():
        pl.semaphore_wait(barrier, LAT - 1 + has_above.astype(jnp.int32) + has_below.astype(jnp.int32))

        def send(step, _):
            peer = lax.bitwise_xor(me, lax.bitwise_xor(step, FAR))
            peer_x, peer_y = peer // 8, lax.rem(peer // 2, 4)
            peer_block = jnp.where(peer_x >= 2, 3 - peer_y // 2, peer_y // 2)
            peer_member = 4 * lax.rem(peer_x, 2) + 2 * lax.rem(peer_y, 2) + lax.rem(peer, 2)
            remote(
                sent_there.at[0, peer_member, block_of(peer_block)],
                got_there.at[0, me], there_send.at[0], there_recv.at[0], (depth, peer),
            ).start()
            return 0

        lax.fori_loop(0, FAR, send, 0)
        lax.fori_loop(FAR + 1, LAT, send, 0)
        got_there[0, me] = sent_there[0, member, level]
        for load in loads[5:]:
            load.wait()
        for z in range(LEVELS):
            slow[z] = OMEGA * (slow[z] - ref_slow[z])
        edge_sent[0] = slow[LEVELS - 1]
        edge_sent[1] = slow[0]
        down = remote(edge_sent.at[0], edge_got.at[0], edge_send.at[0], edge_recv.at[0], (depth + 1, me))
        up = remote(edge_sent.at[1], edge_got.at[1], edge_send.at[1], edge_recv.at[1], (depth - 1, me))

        @pl.when(has_below)
        def _():
            down.start()

        @pl.when(has_above)
        def _():
            up.start()

        for z in range(LEVELS - 1):
            context[1, z + 1, 0] = slow[z]
            context[1, z, 1] = slow[z + 1]
        mine = ref_slow[0]
        for z in range(1, LEVELS):
            mine = jnp.where(level == z, ref_slow[z], mine)
        mult[0], mult[1] = multiplier(member, mine)
        nothing = jnp.zeros((ROWS, N), jnp.float32)

        @pl.when(has_above)
        def _():
            down.wait_recv()
            context[1, 0, 0] = edge_got[0]

        @pl.when(jnp.logical_not(has_above))
        def _():
            context[1, 0, 0] = nothing

        @pl.when(has_below)
        def _():
            up.wait_recv()
            context[1, LEVELS - 1, 1] = edge_got[1]

        @pl.when(jnp.logical_not(has_below))
        def _():
            context[1, LEVELS - 1, 1] = nothing

        holder = me // LEVELS
        place = lax.rem(me, LEVELS)
        for z in range(LEVELS):
            target = device_of(block_of(z), holder)

            @pl.when(target != me)
            def _():
                remote(
                    context.at[1, z], context.at[0, place], context_send, context_recv, (depth, target)
                ).start()

            @pl.when(target == me)
            def _():
                context[0, place] = context[1, z]

        @pl.when(jnp.logical_not(has_above))
        def _():
            target = device_of(0, holder)

            @pl.when(target != me)
            def _():
                remote(
                    source.at[0], source.at[1 + place], source_send, source_recv, (depth, target)
                ).start()

            @pl.when(target == me)
            def _():
                source[1 + place] = source[0]

    def later_there(tick):
        def send(step, _):
            peer = lax.bitwise_xor(member, GROUP - step)
            remote(
                sent_there.at[tick, peer], got_there.at[tick, pl.ds(LEVELS * member, LEVELS)],
                there_send.at[tick], there_recv.at[tick], (depth, device_of(block, peer)),
            ).start()
            return 0

        lax.fori_loop(1, GROUP, send, 0)
        got_there[tick, pl.ds(LEVELS * member, LEVELS)] = sent_there[tick, member]

    def far_member(to_block):
        across = (to_block // 2) != (block // 2)
        return jnp.where(to_block == block, 6, jnp.where(across, 2, 4))

    def group_back(tick):
        is_last = level == LEVELS - 1
        is_first = level == 0
        down_depth = depth + is_last.astype(jnp.int32)
        up_depth = depth - is_first.astype(jnp.int32)
        forth = jnp.where(flipped == 1, -1, 1)
        down_block = block + jnp.where(is_last, 0, forth)
        up_block = block - jnp.where(is_first, 0, forth)
        goes_down = jnp.logical_or(has_below, jnp.logical_not(is_last))
        goes_up = jnp.logical_or(has_above, jnp.logical_not(is_first))
        sides = (
            (0, goes_down, down_depth, down_block, far_member(down_block)),
            (1, goes_up, up_depth, up_block, far_member(up_block)),
        )

        def send(step, _):
            for side, goes, to_depth, to_block, far in sides:
                @pl.when(goes)
                def _():
                    peer = lax.bitwise_xor(member, lax.bitwise_xor(step, far))
                    remote(
                        sent_back.at[tick, pl.ds(LAT // 2 * side + 2 * peer, 2)],
                        got_back.at[tick, side, pl.ds(2 * member, 2)],
                        back_send.at[tick, side], back_recv.at[tick, side],
                        (to_depth, device_of(to_block, peer)),
                    ).start()

            return 0

        lax.fori_loop(0, GROUP, send, 0)
        return goes_down, goes_up

    def group_back_waits(tick, side):
        return remote(
            sent_back.at[tick, pl.ds(LAT // 2 * side, LAT // 2)], got_back.at[tick, side],
            back_send.at[tick, side], back_recv.at[tick, side], neighbour,
        )

    def last_waits(side, count, to):
        return remote(
            sent_back.at[last, pl.ds(0, count)], got_last.at[pl.ds(to, count)],
            last_send.at[side], last_recv.at[side], neighbour,
        )

    def one_tick(tick, _):
        real = state[0].reshape(HALF, N)
        imag = state[1].reshape(HALF, N)
        real, imag = along_y(real, imag, rows, -1)
        sent_there[tick] = to_tiles(real, imag, roll)

        @pl.when(tick == 0)
        def _():
            first_there()
            remote(
                got_there.at[0, pl.ds(0, LAT - 1)], got_there.at[0, pl.ds(0, LAT - 1)],
                there_send.at[0], there_recv.at[0], neighbour,
            ).wait_recv()

        @pl.when(tick > 0)
        def _():
            later_there(tick)
            remote(
                got_there.at[tick, pl.ds(0, LAT - LEVELS)],
                got_there.at[tick, pl.ds(0, LAT - LEVELS)],
                there_send.at[tick], there_recv.at[tick], neighbour,
            ).wait_recv()

        x = got_there[tick].reshape(N, LANES)
        x = middle(x, mult[0], mult[1], columns, roll).reshape(LAT, ROWS, LANES)

        @pl.when(tick < last)
        def _():
            pairs = x.reshape(LAT // 2, 2, ROWS, LANES)
            down, up = packed(pairs[:, 0], pairs[:, 1], roll)
            sent_back[tick, : LAT // 2] = down
            sent_back[tick, LAT // 2 :] = up
            goes = group_back(tick)

            def fill(which):
                angle = context[which, :, 0:2]
                corr[which, 0] = jnp.cos(angle)
                corr[which, 1] = jnp.sin(angle)

            @pl.when(tick == 0)
            def _():
                here = me // LEVELS == member
                for count in (LEVELS - 1, LEVELS):
                    @pl.when(here == (count < LEVELS))
                    def _():
                        remote(
                            context.at[1, pl.ds(0, count)], context.at[0, pl.ds(0, count)],
                            context_send, context_recv, neighbour,
                        ).wait_recv()

                    @pl.when(jnp.logical_and(jnp.logical_not(has_above), block == 0))
                    def _():
                        @pl.when(here == (count < LEVELS))
                        def _():
                            remote(
                                source.at[pl.ds(0, count)], source.at[pl.ds(1, count)],
                                source_send, source_recv, neighbour,
                            ).wait_recv()

                fill(0)

            @pl.when(tick == 1)
            def _():
                fill(1)

            comes_down = jnp.logical_or(has_above, level > 0)
            comes_up = jnp.logical_or(has_below, level < LEVELS - 1)
            for side, comes in ((0, comes_down), (1, comes_up)):
                @pl.when(comes)
                def _():
                    group_back_waits(tick, side).wait_recv()

                @pl.when(jnp.logical_not(comes))
                def _():
                    got_back[tick, side] = jnp.zeros((LAT // 2, ROWS, LANES), jnp.float32)

            down = got_back[tick, 0].reshape(GROUP, 2, ROWS, LANES)
            up = got_back[tick, 1].reshape(GROUP, 2, ROWS, LANES)
            for du, got in enumerate((down, up)):
                for part, piece in enumerate(from_pairs(got, roll)):
                    state[part, :, du] = piece
            for side in range(2):
                @pl.when(goes[side])
                def _():
                    group_back_waits(tick, side).wait_send()

        @pl.when(tick == last)
        def _():
            sent_back[last] = x
            slot = level * GROUP + member

            goes_down = jnp.logical_and(level == LEVELS - 1, has_below)
            goes_up = jnp.logical_and(level == 0, has_above)

            def send(step, _):
                peer = lax.bitwise_xor(me, lax.bitwise_xor(step, FAR))

                def push(side, where, place):
                    remote(
                        sent_back.at[last, peer], got_last.at[place],
                        last_send.at[side], last_recv.at[side], (where, peer),
                    ).start()

                @pl.when(goes_down)
                def _():
                    push(1, depth + 1, LAT + member)

                @pl.when(goes_up)
                def _():
                    push(2, depth - 1, LAT + GROUP + member)

                @pl.when(peer != me)
                def _():
                    push(0, depth, slot)

                return 0

            lax.fori_loop(0, LAT, send, 0)
            got_last[slot] = sent_back[last, me]
            for side, comes, place in ((1, has_above, LAT), (2, has_below, LAT + GROUP)):
                @pl.when(comes)
                def _():
                    last_waits(side, GROUP, place).wait_recv()

                @pl.when(jnp.logical_not(comes))
                def _():
                    got_last[pl.ds(place, GROUP)] = jnp.zeros((GROUP, ROWS, LANES), jnp.float32)

            last_waits(0, LAT - 1, 0).wait_recv()
            down = is_down((GROUP, ROWS, LANES))
            for z in range(LEVELS):
                above = GROUP * (z - 1) if z > 0 else LAT
                below = GROUP * (z + 1) if z < LEVELS - 1 else LAT + GROUP
                got = jnp.where(down, got_last[above : above + GROUP], got_last[below : below + GROUP])
                for n, piece in enumerate(from_tiles(got, roll)):
                    state[n // 2, z, n % 2] = piece
            last_waits(0, LAT - 1, 0).wait_send()
            for side, goes in ((1, goes_down), (2, goes_up)):
                @pl.when(goes)
                def _():
                    last_waits(side, LAT, 0).wait_send()

        real, imag = along_y(state[0].reshape(HALF, N), state[1].reshape(HALF, N), rows, 1)
        real = real.reshape(LEVELS, 2, ROWS, N)
        imag = imag.reshape(LEVELS, 2, ROWS, N)
        at_end = (tick == last).astype(jnp.int32)
        for g in range(LEVELS):
            heads = jnp.logical_and(jnp.logical_not(has_above), jnp.where(tick == last, g, level) == 0)
            tails = jnp.logical_and(
                jnp.logical_not(has_below), jnp.where(tick == last, g, level) == LEVELS - 1
            )
            origin = source[jnp.where(tick == last, 0, 1 + g)]
            parts = mixed(
                real[g], imag[g], corr[at_end, :, g], context[at_end, g, 2], heads, tails, origin
            )
            for part in range(2):
                state[part, g, 0], state[part, g, 1] = parts[part]
        return 0

    lax.fori_loop(0, TICKS, one_tick, 0)
    remote(
        got_there.at[0, pl.ds(0, LAT - 1)], got_there.at[0, pl.ds(0, LAT - 1)],
        there_send.at[0], there_recv.at[0], neighbour,
    ).wait_send()
    for tick in range(1, TICKS):
        remote(
            got_there.at[tick, pl.ds(0, LAT - LEVELS)], got_there.at[tick, pl.ds(0, LAT - LEVELS)],
            there_send.at[tick], there_recv.at[tick], neighbour,
        ).wait_send()
    holder = me // LEVELS
    here = holder == member
    for count in (LEVELS - 1, LEVELS):
        @pl.when(here == (count < LEVELS))
        def _():
            remote(
                context.at[1, pl.ds(0, count)], context.at[0, pl.ds(0, count)],
                context_send, context_recv, neighbour,
            ).wait_send()

    @pl.when(jnp.logical_and(jnp.logical_not(has_above), device_of(0, holder) != me))
    def _():
        remote(source.at[0], source.at[1], source_send, source_recv, neighbour).wait_send()

    for side, goes in ((0, has_below), (1, has_above)):
        @pl.when(goes)
        def _():
            remote(
                edge_sent.at[side], edge_got.at[side], edge_send.at[side], edge_recv.at[side], neighbour
            ).wait_send()


def handed_out(state, out_dr, out_di, out_ur, out_ui, sems):
    copies = [
        pltpu.make_async_copy(state.at[n % 2, :, n // 2], out, sems.at[n])
        for n, out in enumerate((out_dr, out_di, out_ur, out_ui))
    ]
    for copy in copies:
        copy.start()
    for copy in copies:
        copy.wait()


def solution(mesh):
    tables = constants()
    plane = jax.ShapeDtypeStruct((LEVELS, ROWS, N), jnp.float32)
    anywhere = pl.BlockSpec(memory_space=pl.ANY)
    smem = pl.BlockSpec(memory_space=pltpu.SMEM)
    whole = pl.BlockSpec(memory_space=pltpu.VMEM)
    f32 = jnp.float32

    def step(*args):
        state = pl.pallas_call(
            kernel,
            out_shape=pltpu.VMEM((2, LEVELS, 2, ROWS, N), f32),
            in_specs=[anywhere] * 5 + [smem] + [anywhere] * 5,
            out_specs=whole,
            scratch_shapes=[
                pltpu.VMEM((LEVELS, ROWS, N), f32),
                pltpu.VMEM((1 + LEVELS, 2, ROWS, N), f32),
                *[pltpu.VMEM(table.shape, jnp.bfloat16) for table in tables],
                pltpu.VMEM((2, N, LANES), f32),
                pltpu.VMEM((2, LEVELS, 3, ROWS, N), f32),
                pltpu.VMEM((2, 2, LEVELS, 2, ROWS, N), f32),
                pltpu.VMEM((TICKS, GROUP, LEVELS, ROWS, LANES), f32),
                pltpu.VMEM((TICKS, LAT, ROWS, LANES), f32),
                pltpu.VMEM((TICKS, LAT, ROWS, LANES), f32),
                pltpu.VMEM((TICKS - 1, 2, LAT // 2, ROWS, LANES), f32),
                pltpu.VMEM((LAT + 2 * GROUP, ROWS, LANES), f32),
                *[pltpu.VMEM((2, ROWS, N), f32)] * 2,
                pltpu.SemaphoreType.DMA((10,)),
                *[pltpu.SemaphoreType.DMA((TICKS,))] * 2,
                *[pltpu.SemaphoreType.DMA((TICKS - 1, 2))] * 2,
                *[pltpu.SemaphoreType.DMA((3,))] * 2,
                *[pltpu.SemaphoreType.DMA((2,))] * 2,
                *[pltpu.SemaphoreType.DMA] * 4,
            ],
            compiler_params=pltpu.CompilerParams(collective_id=0, has_side_effects=True),
        )(*args, *[jnp.asarray(table) for table in tables])
        return pl.pallas_call(
            handed_out,
            out_shape=[plane] * 4,
            in_specs=[whole],
            out_specs=[anywhere] * 4,
            scratch_shapes=[pltpu.SemaphoreType.DMA((4,))],
            compiler_params=pltpu.CompilerParams(vmem_limit_bytes=2**20),
        )(state)

    lateral = P("depth", "lat", None)
    return jax.shard_map(
        step,
        mesh=mesh,
        in_specs=(lateral,) * 5 + (P("depth"), lateral, P("lat", None), P("lat", None)),
        out_specs=(lateral,) * 4,
        check_vma=False,
    )
```

```python
import math

import jax
import jax.numpy as jnp
import ml_dtypes
import numpy as np
from jax import lax
from jax.experimental import pallas as pl
from jax.experimental.pallas import tpu as pltpu
from jax.sharding import PartitionSpec as P

TICKS = 3
OMEGA = 2.5
MESH = pl.DeviceIdType.MESH

LEVELS = 4
GROUP = 8
LAT = 32
FAR = 20
ROWS = 8
N = 256
LANES = 128
HALF = 64
HALVES = N // 2
WAVES = N // GROUP


def split(x):
    high = x.astype(jnp.bfloat16)
    low = (x - high.astype(jnp.float32)).astype(jnp.bfloat16)
    return high, low


def np_split(x):
    x = np.asarray(x, np.float64)
    high = x.astype(np.float32).astype(ml_dtypes.bfloat16)
    low = (x - high.astype(np.float64)).astype(np.float32).astype(ml_dtypes.bfloat16)
    return high, low


def constants():
    index = np.arange(HALVES)
    angles = (
        2.0 * np.pi * (np.outer(2 * index, index) % N) / N,
        2.0 * np.pi * (np.outer(2 * index + 1, index) % N) / N,
    )
    even, odd = angles
    by_row = []
    for angle in (even, odd.T, odd):
        for part in np_split(np.concatenate([np.cos(angle), np.sin(angle)], axis=1)):
            by_row.append(np.concatenate([part, part], axis=0))
    by_column = []
    for angle in (even, odd, odd.T):
        by_column.extend(np_split(np.concatenate([np.cos(angle), np.sin(angle)], axis=0)))
    return np.stack(by_row), np.stack(by_column)


def dot(a, b, dims=((1,), (0,))):
    return lax.dot_general(a, b, (dims, ((), ())), preferred_element_type=jnp.float32)


def lanes(shape):
    return lax.broadcasted_iota(jnp.int32, shape, len(shape) - 1)


def block_swap(tiles, roll):
    block = lanes(tiles[0].shape) // WAVES
    for bit in (2, 1):
        keep = (block & bit) == 0
        shift = bit * WAVES
        new = list(tiles)
        for a in range(4):
            if a & bit == 0:
                low, high = tiles[a], tiles[a + bit]
                new[a] = jnp.where(keep, low, roll(high, shift))
                new[a + bit] = jnp.where(keep, roll(low, LANES - shift), high)
        tiles = new
    return tiles


def along_y(real, imag, rows, sign):
    x = jnp.concatenate([real, imag], axis=0)
    first, second = x[:, :HALVES], x[:, HALVES:]
    if sign < 0:
        first, second = first + second, first - second
    out = []
    for table, part in ((0, first), (2 if sign < 0 else 4, second)):
        both = jnp.concatenate(split(part), axis=1)
        total = dot(both, rows[table]) + dot(both, rows[table + 1])
        cosine, sine = total[:, :HALVES], total[:, HALVES:]
        if sign < 0:
            out.append((cosine[:HALF] + sine[HALF:], cosine[HALF:] - sine[:HALF]))
        else:
            out.append((cosine[:HALF] - sine[HALF:], cosine[HALF:] + sine[:HALF]))
    parts = []
    for first, second in zip(*out):
        if sign > 0:
            first, second = first + second, first - second
        parts.append(jnp.concatenate([first, second], axis=1))
    return parts


def to_tiles(real, imag, roll):
    parts = [x.reshape(LEVELS, 2, ROWS, N) for x in (real, imag)]
    rows = [parts[c][:, du] for c in range(2) for du in range(2)]
    halves = [block_swap([x[:, :, LANES * h : LANES * (h + 1)] for x in rows], roll) for h in range(2)]
    return jnp.stack([halves[h][b] for h in range(2) for b in range(4)])


def from_tiles(x, roll):
    halves = [block_swap([x[4 * h + a] for a in range(4)], roll) for h in range(2)]
    return [jnp.concatenate([halves[0][b], halves[1][b]], axis=-1) for b in range(4)]


def from_pairs(x, roll):
    rows = [from_tiles(x[:, j], roll) for j in range(2)]
    return [jnp.stack([rows[g // 2][2 * part + g % 2] for g in range(LEVELS)]) for part in range(2)]


def signs(shape):
    return jnp.where(lanes(shape) < HALF, 1.0, -1.0).astype(jnp.float32)


def along_x(x, columns, sign, roll):
    first, second = x[:HALVES], x[HALVES:]
    if sign < 0:
        first, second = first + second, first - second
    turn = -sign * signs((HALVES, LANES))
    out = []
    for table, part in ((0, first), (2 if sign < 0 else 4, second)):
        high, low = split(part)
        wide = dot(columns[table], jnp.concatenate([high, low], axis=1))
        total = wide[:, :LANES] + (wide[:, LANES:] + dot(columns[table + 1], high))
        out.append(total[:HALVES] + turn * roll(total[HALVES:], HALF))
    first, second = out
    if sign > 0:
        first, second = first + second, first - second
    return jnp.concatenate([first, second], axis=0)


def turned(x, cosine, sine, roll):
    return x * cosine + roll(x, HALF) * sine


def middle(x, mult_real, mult_imag, columns, roll):
    x = along_x(x, columns, -1, roll)
    x = turned(x, mult_real, mult_imag, roll)
    return along_x(x, columns, 1, roll)


def is_down(shape):
    return (lanes(shape) // WAVES) % 2 == 0


def packed(even, odd, roll):
    down = is_down(even.shape)
    return jnp.where(down, even, roll(odd, WAVES)), jnp.where(down, roll(even, LANES - WAVES), odd)


def wrapped_numbers(index):
    folded = jnp.where(index < N // 2, index, index - N)
    return folded.astype(jnp.float32) * (2.0 * math.pi / N)


def in_order(place):
    return jnp.where(place < HALVES, 2 * place, 2 * (place - HALVES) + 1)


def multiplier(member, slow):
    row = lax.broadcasted_iota(jnp.int32, (N, LANES), 0)
    lane = lax.broadcasted_iota(jnp.int32, (N, LANES), 1)
    wave_x = wrapped_numbers(in_order(row))
    wave_y = wrapped_numbers(in_order(WAVES * member + lane % WAVES))
    argument = (OMEGA * slow) ** 2 - (wave_x * wave_x + wave_y * wave_y)
    vertical = jnp.sqrt(jnp.maximum(argument, 0.0))
    factor = jnp.exp(-jnp.sqrt(jnp.maximum(-argument, 0.0))) * (1.0 / (N * N))
    return factor * jnp.cos(vertical), signs((N, LANES)) * (factor * jnp.sin(vertical))


def mixed(real, imag, corr, refl, heads, tails, source):
    out = []
    for part in range(2):
        if part == 0:
            prop = real * corr[0] + imag * corr[1]
        else:
            prop = imag * corr[0] - real * corr[1]
        down = jnp.where(heads, source[part], prop[0])
        up = jnp.where(tails, 0.0, prop[1])
        out.append((down - refl * up, up + refl * down))
    return out


def kernel(
    down_real, down_imag, up_real, up_imag, slowness, ref_slow, reflect, source_real, source_imag,
    rows_hbm, columns_hbm, state,
    slow, source, rows, columns,
    mult, context, corr, sent_there, got_there, sent_back, got_back, got_last, edge_sent, edge_got,
    in_sems, there_send, there_recv, back_send, back_recv, last_send, last_recv,
    edge_send, edge_recv, context_send, context_recv, source_send, source_recv,
):
    me = lax.axis_index("lat")
    depth = lax.axis_index("depth")
    depths = lax.axis_size("depth")
    cell_x, cell_y, core = me // 8, lax.rem(me // 2, 4), lax.rem(me, 2)
    member = 4 * lax.rem(cell_x, 2) + 2 * lax.rem(cell_y, 2) + core
    block = jnp.where(cell_x >= 2, 3 - cell_y // 2, cell_y // 2)
    flipped = lax.rem(depth, 2)
    level = jnp.where(flipped == 1, LEVELS - 1 - block, block)
    has_above = depth > 0
    has_below = depth < depths - 1
    last = TICKS - 1

    def block_of(z):
        return jnp.where(flipped == 1, LEVELS - 1 - z, z)

    def device_of(block, member):
        block_x, block_y = block // 2, lax.rem(block + 1, 4) // 2
        return 16 * block_x + 4 * block_y + 8 * (member // 4) + lax.rem(member, 4)

    def roll(x, shift):
        return pltpu.roll(x, shift, x.ndim - 1)

    def remote(src, dst, send_sem, recv_sem, where):
        return pltpu.make_async_remote_copy(
            src_ref=src, dst_ref=dst, send_sem=send_sem, recv_sem=recv_sem,
            device_id=where, device_id_type=MESH,
        )

    neighbour = (depth, lax.bitwise_xor(me, 1))

    loads = [
        pltpu.make_async_copy(src, dst, in_sems.at[n])
        for n, (src, dst) in enumerate([
            (down_real, state.at[0, :, 0]), (up_real, state.at[0, :, 1]),
            (down_imag, state.at[1, :, 0]), (up_imag, state.at[1, :, 1]),
            (rows_hbm, rows), (slowness, slow), (reflect, context.at[1, :, 2]),
            (source_real, source.at[0, 0]), (source_imag, source.at[0, 1]),
            (columns_hbm, columns),
        ])
    ]
    barrier = pltpu.get_barrier_semaphore()

    def greet(step, _):
        peer = lax.bitwise_xor(me, lax.bitwise_xor(step, FAR))
        pl.semaphore_signal(barrier, inc=1, device_id=(depth, peer), device_id_type=MESH)
        return 0

    lax.fori_loop(0, FAR, greet, 0)
    lax.fori_loop(FAR + 1, LAT, greet, 0)

    @pl.when(has_above)
    def _():
        pl.semaphore_signal(barrier, inc=1, device_id=(depth - 1, me), device_id_type=MESH)

    @pl.when(has_below)
    def _():
        pl.semaphore_signal(barrier, inc=1, device_id=(depth + 1, me), device_id_type=MESH)

    for load in loads:
        load.start()

    for load in loads[:5]:
        load.wait()

    def first_there():
        for load in loads[5:]:
            load.wait()
        for z in range(LEVELS):
            slow[z] = OMEGA * (slow[z] - ref_slow[z])
        edge_sent[0] = slow[LEVELS - 1]
        edge_sent[1] = slow[0]
        for z in range(LEVELS - 1):
            context[1, z + 1, 0] = slow[z]
            context[1, z, 1] = slow[z + 1]
        pl.semaphore_wait(barrier, LAT - 1 + has_above.astype(jnp.int32) + has_below.astype(jnp.int32))
        down = remote(edge_sent.at[0], edge_got.at[0], edge_send.at[0], edge_recv.at[0], (depth + 1, me))
        up = remote(edge_sent.at[1], edge_got.at[1], edge_send.at[1], edge_recv.at[1], (depth - 1, me))

        @pl.when(has_below)
        def _():
            down.start()

        @pl.when(has_above)
        def _():
            up.start()

        def send(step, _):
            peer = lax.bitwise_xor(me, lax.bitwise_xor(step, FAR))
            peer_x, peer_y = peer // 8, lax.rem(peer // 2, 4)
            peer_block = jnp.where(peer_x >= 2, 3 - peer_y // 2, peer_y // 2)
            peer_member = 4 * lax.rem(peer_x, 2) + 2 * lax.rem(peer_y, 2) + lax.rem(peer, 2)
            remote(
                sent_there.at[0, peer_member, block_of(peer_block)],
                got_there.at[0, me], there_send.at[0], there_recv.at[0], (depth, peer),
            ).start()
            return 0

        lax.fori_loop(0, FAR, send, 0)
        lax.fori_loop(FAR + 1, LAT, send, 0)
        got_there[0, me] = sent_there[0, member, level]
        mine = ref_slow[0]
        for z in range(1, LEVELS):
            mine = jnp.where(level == z, ref_slow[z], mine)
        mult[0], mult[1] = multiplier(member, mine)
        nothing = jnp.zeros((ROWS, N), jnp.float32)

        @pl.when(has_above)
        def _():
            down.wait_recv()
            context[1, 0, 0] = edge_got[0]

        @pl.when(jnp.logical_not(has_above))
        def _():
            context[1, 0, 0] = nothing

        @pl.when(has_below)
        def _():
            up.wait_recv()
            context[1, LEVELS - 1, 1] = edge_got[1]

        @pl.when(jnp.logical_not(has_below))
        def _():
            context[1, LEVELS - 1, 1] = nothing

        holder = me // LEVELS
        place = lax.rem(me, LEVELS)
        for z in range(LEVELS):
            target = device_of(block_of(z), holder)

            @pl.when(target != me)
            def _():
                remote(
                    context.at[1, z], context.at[0, place], context_send, context_recv, (depth, target)
                ).start()

            @pl.when(target == me)
            def _():
                context[0, place] = context[1, z]

        @pl.when(jnp.logical_not(has_above))
        def _():
            target = device_of(0, holder)

            @pl.when(target != me)
            def _():
                remote(
                    source.at[0], source.at[1 + place], source_send, source_recv, (depth, target)
                ).start()

            @pl.when(target == me)
            def _():
                source[1 + place] = source[0]

    def later_there(tick):
        def send(step, _):
            peer = lax.bitwise_xor(member, GROUP - step)
            remote(
                sent_there.at[tick, peer], got_there.at[tick, pl.ds(LEVELS * member, LEVELS)],
                there_send.at[tick], there_recv.at[tick], (depth, device_of(block, peer)),
            ).start()
            return 0

        lax.fori_loop(1, GROUP, send, 0)
        got_there[tick, pl.ds(LEVELS * member, LEVELS)] = sent_there[tick, member]

    def far_member(to_block):
        across = (to_block // 2) != (block // 2)
        return jnp.where(to_block == block, 6, jnp.where(across, 2, 4))

    def group_back(tick):
        is_last = level == LEVELS - 1
        is_first = level == 0
        down_depth = depth + is_last.astype(jnp.int32)
        up_depth = depth - is_first.astype(jnp.int32)
        forth = jnp.where(flipped == 1, -1, 1)
        down_block = block + jnp.where(is_last, 0, forth)
        up_block = block - jnp.where(is_first, 0, forth)
        goes_down = jnp.logical_or(has_below, jnp.logical_not(is_last))
        goes_up = jnp.logical_or(has_above, jnp.logical_not(is_first))
        sides = (
            (0, goes_down, down_depth, down_block, far_member(down_block)),
            (1, goes_up, up_depth, up_block, far_member(up_block)),
        )

        def send(step, _):
            for side, goes, to_depth, to_block, far in sides:
                @pl.when(goes)
                def _():
                    peer = lax.bitwise_xor(member, lax.bitwise_xor(step, far))
                    remote(
                        sent_back.at[tick, pl.ds(LAT // 2 * side + 2 * peer, 2)],
                        got_back.at[tick, side, pl.ds(2 * member, 2)],
                        back_send.at[tick, side], back_recv.at[tick, side],
                        (to_depth, device_of(to_block, peer)),
                    ).start()

            return 0

        lax.fori_loop(0, GROUP, send, 0)

    def group_back_waits(tick, side):
        return remote(
            sent_back.at[tick, pl.ds(LAT // 2 * side, LAT // 2)], got_back.at[tick, side],
            back_send.at[tick, side], back_recv.at[tick, side], neighbour,
        )

    def last_waits(side, count, to):
        return remote(
            sent_back.at[last, pl.ds(0, count)], got_last.at[pl.ds(to, count)],
            last_send.at[side], last_recv.at[side], neighbour,
        )

    def one_tick(tick, _):
        real = state[0].reshape(HALF, N)
        imag = state[1].reshape(HALF, N)
        real, imag = along_y(real, imag, rows, -1)
        sent_there[tick] = to_tiles(real, imag, roll)

        @pl.when(tick == 0)
        def _():
            first_there()
            remote(
                got_there.at[0, pl.ds(0, LAT - 1)], got_there.at[0, pl.ds(0, LAT - 1)],
                there_send.at[0], there_recv.at[0], neighbour,
            ).wait_recv()

        @pl.when(tick > 0)
        def _():
            later_there(tick)
            remote(
                got_there.at[tick, pl.ds(0, LAT - LEVELS)],
                got_there.at[tick, pl.ds(0, LAT - LEVELS)],
                there_send.at[tick], there_recv.at[tick], neighbour,
            ).wait_recv()

        x = got_there[tick].reshape(N, LANES)
        x = middle(x, mult[0], mult[1], columns, roll).reshape(LAT, ROWS, LANES)

        @pl.when(tick < last)
        def _():
            pairs = x.reshape(LAT // 2, 2, ROWS, LANES)
            down, up = packed(pairs[:, 0], pairs[:, 1], roll)
            sent_back[tick, : LAT // 2] = down
            sent_back[tick, LAT // 2 :] = up
            group_back(tick)

            def fill(which):
                angle = context[which, :, 0:2]
                corr[which, 0] = jnp.cos(angle)
                corr[which, 1] = jnp.sin(angle)

            @pl.when(tick == 0)
            def _():
                here = me // LEVELS == member
                for count in (LEVELS - 1, LEVELS):
                    @pl.when(here == (count < LEVELS))
                    def _():
                        remote(
                            context.at[1, pl.ds(0, count)], context.at[0, pl.ds(0, count)],
                            context_send, context_recv, neighbour,
                        ).wait_recv()

                    @pl.when(jnp.logical_and(jnp.logical_not(has_above), block == 0))
                    def _():
                        @pl.when(here == (count < LEVELS))
                        def _():
                            remote(
                                source.at[pl.ds(0, count)], source.at[pl.ds(1, count)],
                                source_send, source_recv, neighbour,
                            ).wait_recv()

                fill(0)

            @pl.when(tick == 1)
            def _():
                fill(1)

            comes_down = jnp.logical_or(has_above, level > 0)
            comes_up = jnp.logical_or(has_below, level < LEVELS - 1)
            for side, comes in ((0, comes_down), (1, comes_up)):
                @pl.when(comes)
                def _():
                    group_back_waits(tick, side).wait_recv()

                @pl.when(jnp.logical_not(comes))
                def _():
                    got_back[tick, side] = jnp.zeros((LAT // 2, ROWS, LANES), jnp.float32)

            down = got_back[tick, 0].reshape(GROUP, 2, ROWS, LANES)
            up = got_back[tick, 1].reshape(GROUP, 2, ROWS, LANES)
            for du, got in enumerate((down, up)):
                for part, piece in enumerate(from_pairs(got, roll)):
                    state[part, :, du] = piece

        @pl.when(tick == last)
        def _():
            sent_back[last] = x
            slot = level * GROUP + member

            goes_down = jnp.logical_and(level == LEVELS - 1, has_below)
            goes_up = jnp.logical_and(level == 0, has_above)

            def send(step, _):
                peer = lax.bitwise_xor(me, lax.bitwise_xor(step, FAR))

                def push(side, where, place):
                    remote(
                        sent_back.at[last, peer], got_last.at[place],
                        last_send.at[side], last_recv.at[side], (where, peer),
                    ).start()

                @pl.when(goes_down)
                def _():
                    push(1, depth + 1, LAT + member)

                @pl.when(goes_up)
                def _():
                    push(2, depth - 1, LAT + GROUP + member)

                @pl.when(peer != me)
                def _():
                    push(0, depth, slot)

                return 0

            lax.fori_loop(0, LAT, send, 0)
            got_last[slot] = sent_back[last, me]
            for side, comes, place in ((1, has_above, LAT), (2, has_below, LAT + GROUP)):
                @pl.when(comes)
                def _():
                    last_waits(side, GROUP, place).wait_recv()

                @pl.when(jnp.logical_not(comes))
                def _():
                    got_last[pl.ds(place, GROUP)] = jnp.zeros((GROUP, ROWS, LANES), jnp.float32)

            last_waits(0, LAT - 1, 0).wait_recv()
            down = is_down((GROUP, ROWS, LANES))
            for z in range(LEVELS):
                above = GROUP * (z - 1) if z > 0 else LAT
                below = GROUP * (z + 1) if z < LEVELS - 1 else LAT + GROUP
                got = jnp.where(down, got_last[above : above + GROUP], got_last[below : below + GROUP])
                for n, piece in enumerate(from_tiles(got, roll)):
                    state[n // 2, z, n % 2] = piece

        real, imag = along_y(state[0].reshape(HALF, N), state[1].reshape(HALF, N), rows, 1)
        real = real.reshape(LEVELS, 2, ROWS, N)
        imag = imag.reshape(LEVELS, 2, ROWS, N)
        at_end = (tick == last).astype(jnp.int32)
        for g in range(LEVELS):
            heads = jnp.logical_and(jnp.logical_not(has_above), jnp.where(tick == last, g, level) == 0)
            tails = jnp.logical_and(
                jnp.logical_not(has_below), jnp.where(tick == last, g, level) == LEVELS - 1
            )
            origin = source[jnp.where(tick == last, 0, 1 + g)]
            parts = mixed(
                real[g], imag[g], corr[at_end, :, g], context[at_end, g, 2], heads, tails, origin
            )
            for part in range(2):
                state[part, g, 0], state[part, g, 1] = parts[part]
        return 0

    lax.fori_loop(0, TICKS, one_tick, 0)
    last_waits(0, LAT - 1, 0).wait_send()
    for side, edge_level, beyond in ((0, LEVELS - 1, has_below), (1, 0, has_above)):
        @pl.when(jnp.logical_or(beyond, level != edge_level))
        def _():
            for tick in range(last):
                group_back_waits(tick, side).wait_send()

        @pl.when(jnp.logical_and(beyond, level == edge_level))
        def _():
            last_waits(1 + side, LAT, 0).wait_send()

    remote(
        got_there.at[0, pl.ds(0, LAT - 1)], got_there.at[0, pl.ds(0, LAT - 1)],
        there_send.at[0], there_recv.at[0], neighbour,
    ).wait_send()
    for tick in range(1, TICKS):
        remote(
            got_there.at[tick, pl.ds(0, LAT - LEVELS)], got_there.at[tick, pl.ds(0, LAT - LEVELS)],
            there_send.at[tick], there_recv.at[tick], neighbour,
        ).wait_send()
    holder = me // LEVELS
    here = holder == member
    for count in (LEVELS - 1, LEVELS):
        @pl.when(here == (count < LEVELS))
        def _():
            remote(
                context.at[1, pl.ds(0, count)], context.at[0, pl.ds(0, count)],
                context_send, context_recv, neighbour,
            ).wait_send()

    @pl.when(jnp.logical_and(jnp.logical_not(has_above), device_of(0, holder) != me))
    def _():
        remote(source.at[0], source.at[1], source_send, source_recv, neighbour).wait_send()

    for side, goes in ((0, has_below), (1, has_above)):
        @pl.when(goes)
        def _():
            remote(
                edge_sent.at[side], edge_got.at[side], edge_send.at[side], edge_recv.at[side], neighbour
            ).wait_send()


def handed_out(state, out_dr, out_di, out_ur, out_ui, sems):
    copies = [
        pltpu.make_async_copy(state.at[n % 2, :, n // 2], out, sems.at[n])
        for n, out in enumerate((out_dr, out_di, out_ur, out_ui))
    ]
    for copy in copies:
        copy.start()
    for copy in copies:
        copy.wait()


def solution(mesh):
    tables = constants()
    plane = jax.ShapeDtypeStruct((LEVELS, ROWS, N), jnp.float32)
    anywhere = pl.BlockSpec(memory_space=pl.ANY)
    smem = pl.BlockSpec(memory_space=pltpu.SMEM)
    whole = pl.BlockSpec(memory_space=pltpu.VMEM)
    f32 = jnp.float32

    def step(*args):
        state = pl.pallas_call(
            kernel,
            out_shape=pltpu.VMEM((2, LEVELS, 2, ROWS, N), f32),
            in_specs=[anywhere] * 5 + [smem] + [anywhere] * 5,
            out_specs=whole,
            scratch_shapes=[
                pltpu.VMEM((LEVELS, ROWS, N), f32),
                pltpu.VMEM((1 + LEVELS, 2, ROWS, N), f32),
                *[pltpu.VMEM(table.shape, jnp.bfloat16) for table in tables],
                pltpu.VMEM((2, N, LANES), f32),
                pltpu.VMEM((2, LEVELS, 3, ROWS, N), f32),
                pltpu.VMEM((2, 2, LEVELS, 2, ROWS, N), f32),
                pltpu.VMEM((TICKS, GROUP, LEVELS, ROWS, LANES), f32),
                pltpu.VMEM((TICKS, LAT, ROWS, LANES), f32),
                pltpu.VMEM((TICKS, LAT, ROWS, LANES), f32),
                pltpu.VMEM((TICKS - 1, 2, LAT // 2, ROWS, LANES), f32),
                pltpu.VMEM((LAT + 2 * GROUP, ROWS, LANES), f32),
                *[pltpu.VMEM((2, ROWS, N), f32)] * 2,
                pltpu.SemaphoreType.DMA((10,)),
                *[pltpu.SemaphoreType.DMA((TICKS,))] * 2,
                *[pltpu.SemaphoreType.DMA((TICKS - 1, 2))] * 2,
                *[pltpu.SemaphoreType.DMA((3,))] * 2,
                *[pltpu.SemaphoreType.DMA((2,))] * 2,
                *[pltpu.SemaphoreType.DMA] * 4,
            ],
            compiler_params=pltpu.CompilerParams(collective_id=0, has_side_effects=True),
        )(*args, *[jnp.asarray(table) for table in tables])
        return pl.pallas_call(
            handed_out,
            out_shape=[plane] * 4,
            in_specs=[whole],
            out_specs=[anywhere] * 4,
            scratch_shapes=[pltpu.SemaphoreType.DMA((4,))],
            compiler_params=pltpu.CompilerParams(vmem_limit_bytes=2**20),
        )(state)

    lateral = P("depth", "lat", None)
    return jax.shard_map(
        step,
        mesh=mesh,
        in_specs=(lateral,) * 5 + (P("depth"), lateral, P("lat", None), P("lat", None)),
        out_specs=(lateral,) * 4,
        check_vma=False,
    )
```

```python
import math

import jax
import jax.numpy as jnp
import ml_dtypes
import numpy as np
from jax import lax
from jax.experimental import pallas as pl
from jax.experimental.pallas import tpu as pltpu
from jax.sharding import PartitionSpec as P

TICKS = 3
OMEGA = 2.5
MESH = pl.DeviceIdType.MESH

LEVELS = 4
GROUP = 8
LAT = 32
FAR = 20
ROWS = 8
N = 256
LANES = 128
HALF = 64
HALVES = N // 2
WAVES = N // GROUP


def split(x):
    high = x.astype(jnp.bfloat16)
    low = (x - high.astype(jnp.float32)).astype(jnp.bfloat16)
    return high, low


def np_split(x):
    x = np.asarray(x, np.float64)
    high = x.astype(np.float32).astype(ml_dtypes.bfloat16)
    low = (x - high.astype(np.float64)).astype(np.float32).astype(ml_dtypes.bfloat16)
    return high, low


def constants():
    index = np.arange(HALVES)
    angles = (
        2.0 * np.pi * (np.outer(2 * index, index) % N) / N,
        2.0 * np.pi * (np.outer(2 * index + 1, index) % N) / N,
    )
    even, odd = angles
    by_row = []
    for angle in (even, odd.T, odd):
        for part in np_split(np.concatenate([np.cos(angle), np.sin(angle)], axis=1)):
            by_row.append(np.concatenate([part, part], axis=0))
    by_column = []
    for angle in (even, odd, odd.T):
        by_column.extend(np_split(np.concatenate([np.cos(angle), np.sin(angle)], axis=0)))
    return np.stack(by_row), np.stack(by_column)


def dot(a, b, dims=((1,), (0,))):
    return lax.dot_general(a, b, (dims, ((), ())), preferred_element_type=jnp.float32)


def lanes(shape):
    return lax.broadcasted_iota(jnp.int32, shape, len(shape) - 1)


def block_swap(tiles, roll):
    block = lanes(tiles[0].shape) // WAVES
    for bit in (2, 1):
        keep = (block & bit) == 0
        shift = bit * WAVES
        new = list(tiles)
        for a in range(4):
            if a & bit == 0:
                low, high = tiles[a], tiles[a + bit]
                new[a] = jnp.where(keep, low, roll(high, shift))
                new[a + bit] = jnp.where(keep, roll(low, LANES - shift), high)
        tiles = new
    return tiles


def along_y(real, imag, rows, sign):
    x = jnp.concatenate([real, imag], axis=0)
    first, second = x[:, :HALVES], x[:, HALVES:]
    if sign < 0:
        first, second = first + second, first - second
    out = []
    for table, part in ((0, first), (2 if sign < 0 else 4, second)):
        both = jnp.concatenate(split(part), axis=1)
        total = dot(both, rows[table]) + dot(both, rows[table + 1])
        cosine, sine = total[:, :HALVES], total[:, HALVES:]
        if sign < 0:
            out.append((cosine[:HALF] + sine[HALF:], cosine[HALF:] - sine[:HALF]))
        else:
            out.append((cosine[:HALF] - sine[HALF:], cosine[HALF:] + sine[:HALF]))
    parts = []
    for first, second in zip(*out):
        if sign > 0:
            first, second = first + second, first - second
        parts.append(jnp.concatenate([first, second], axis=1))
    return parts


def to_tiles(real, imag, roll):
    parts = [x.reshape(LEVELS, 2, ROWS, N) for x in (real, imag)]
    rows = [parts[c][:, du] for c in range(2) for du in range(2)]
    halves = [block_swap([x[:, :, LANES * h : LANES * (h + 1)] for x in rows], roll) for h in range(2)]
    return jnp.stack([halves[h][b] for h in range(2) for b in range(4)])


def from_tiles(x, roll):
    halves = [block_swap([x[4 * h + a] for a in range(4)], roll) for h in range(2)]
    return [jnp.concatenate([halves[0][b], halves[1][b]], axis=-1) for b in range(4)]


def from_pairs(x, roll):
    rows = [from_tiles(x[:, j], roll) for j in range(2)]
    return [jnp.stack([rows[g // 2][2 * part + g % 2] for g in range(LEVELS)]) for part in range(2)]


def signs(shape):
    return jnp.where(lanes(shape) < HALF, 1.0, -1.0).astype(jnp.float32)


def along_x(x, columns, sign, roll):
    first, second = x[:HALVES], x[HALVES:]
    if sign < 0:
        first, second = first + second, first - second
    turn = -sign * signs((HALVES, LANES))
    out = []
    for table, part in ((0, first), (2 if sign < 0 else 4, second)):
        high, low = split(part)
        wide = dot(columns[table], jnp.concatenate([high, low], axis=1))
        total = wide[:, :LANES] + (wide[:, LANES:] + dot(columns[table + 1], high))
        out.append(total[:HALVES] + turn * roll(total[HALVES:], HALF))
    first, second = out
    if sign > 0:
        first, second = first + second, first - second
    return jnp.concatenate([first, second], axis=0)


def turned(x, cosine, sine, roll):
    return x * cosine + roll(x, HALF) * sine


def middle(x, mult_real, mult_imag, columns, roll):
    x = along_x(x, columns, -1, roll)
    x = turned(x, mult_real, mult_imag, roll)
    return along_x(x, columns, 1, roll)


def is_down(shape):
    return (lanes(shape) // WAVES) % 2 == 0


def packed(even, odd, roll):
    down = is_down(even.shape)
    return jnp.where(down, even, roll(odd, WAVES)), jnp.where(down, roll(even, LANES - WAVES), odd)


def wrapped_numbers(index):
    folded = jnp.where(index < N // 2, index, index - N)
    return folded.astype(jnp.float32) * (2.0 * math.pi / N)


def in_order(place):
    return jnp.where(place < HALVES, 2 * place, 2 * (place - HALVES) + 1)


def multiplier(member, slow):
    row = lax.broadcasted_iota(jnp.int32, (N, LANES), 0)
    lane = lax.broadcasted_iota(jnp.int32, (N, LANES), 1)
    wave_x = wrapped_numbers(in_order(row))
    wave_y = wrapped_numbers(in_order(WAVES * member + lane % WAVES))
    argument = (OMEGA * slow) ** 2 - (wave_x * wave_x + wave_y * wave_y)
    vertical = jnp.sqrt(jnp.maximum(argument, 0.0))
    factor = jnp.exp(-jnp.sqrt(jnp.maximum(-argument, 0.0))) * (1.0 / (N * N))
    return factor * jnp.cos(vertical), signs((N, LANES)) * (factor * jnp.sin(vertical))


def mixed(real, imag, corr, refl, heads, tails, source):
    out = []
    for part in range(2):
        if part == 0:
            prop = real * corr[0] + imag * corr[1]
        else:
            prop = imag * corr[0] - real * corr[1]
        down = jnp.where(heads, source[part], prop[0])
        up = jnp.where(tails, 0.0, prop[1])
        out.append((down - refl * up, up + refl * down))
    return out


def kernel(
    down_real, down_imag, up_real, up_imag, slowness, ref_slow, reflect, source_real, source_imag,
    rows_hbm, columns_hbm, state,
    slow, source, rows, columns,
    mult, context, corr, sent_there, got_there, sent_back, got_back, got_last, edge_sent, edge_got,
    in_sems, there_send, there_recv, back_send, back_recv, last_send, last_recv,
    edge_send, edge_recv, context_send, context_recv, source_send, source_recv,
):
    me = lax.axis_index("lat")
    depth = lax.axis_index("depth")
    depths = lax.axis_size("depth")
    cell_x, cell_y, core = me // 8, lax.rem(me // 2, 4), lax.rem(me, 2)
    member = 4 * lax.rem(cell_x, 2) + 2 * lax.rem(cell_y, 2) + core
    block = jnp.where(cell_x >= 2, 3 - cell_y // 2, cell_y // 2)
    flipped = lax.rem(depth, 2)
    level = jnp.where(flipped == 1, LEVELS - 1 - block, block)
    has_above = depth > 0
    has_below = depth < depths - 1
    last = TICKS - 1

    def block_of(z):
        return jnp.where(flipped == 1, LEVELS - 1 - z, z)

    def device_of(block, member):
        block_x, block_y = block // 2, lax.rem(block + 1, 4) // 2
        return 16 * block_x + 4 * block_y + 8 * (member // 4) + lax.rem(member, 4)

    def roll(x, shift):
        return pltpu.roll(x, shift, x.ndim - 1)

    def remote(src, dst, send_sem, recv_sem, where):
        return pltpu.make_async_remote_copy(
            src_ref=src, dst_ref=dst, send_sem=send_sem, recv_sem=recv_sem,
            device_id=where, device_id_type=MESH,
        )

    neighbour = (depth, lax.bitwise_xor(me, 1))

    loads = [
        pltpu.make_async_copy(src, dst, in_sems.at[n])
        for n, (src, dst) in enumerate([
            (down_real, state.at[0, :, 0]), (up_real, state.at[0, :, 1]),
            (down_imag, state.at[1, :, 0]), (up_imag, state.at[1, :, 1]),
            (rows_hbm, rows), (slowness, slow), (reflect, context.at[1, :, 2]),
            (source_real, source.at[0, 0]), (source_imag, source.at[0, 1]),
            (columns_hbm, columns),
        ])
    ]
    for load in loads:
        load.start()

    barrier = pltpu.get_barrier_semaphore()

    def greet(step, _):
        peer = lax.bitwise_xor(me, lax.bitwise_xor(step, FAR))
        pl.semaphore_signal(barrier, inc=1, device_id=(depth, peer), device_id_type=MESH)
        return 0

    lax.fori_loop(0, FAR, greet, 0)
    lax.fori_loop(FAR + 1, LAT, greet, 0)

    @pl.when(has_above)
    def _():
        pl.semaphore_signal(barrier, inc=1, device_id=(depth - 1, me), device_id_type=MESH)

    @pl.when(has_below)
    def _():
        pl.semaphore_signal(barrier, inc=1, device_id=(depth + 1, me), device_id_type=MESH)

    for load in loads[:5]:
        load.wait()

    def first_there():
        pl.semaphore_wait(barrier, LAT - 1 + has_above.astype(jnp.int32) + has_below.astype(jnp.int32))

        def send(step, _):
            peer = lax.bitwise_xor(me, lax.bitwise_xor(step, FAR))
            peer_x, peer_y = peer // 8, lax.rem(peer // 2, 4)
            peer_block = jnp.where(peer_x >= 2, 3 - peer_y // 2, peer_y // 2)
            peer_member = 4 * lax.rem(peer_x, 2) + 2 * lax.rem(peer_y, 2) + lax.rem(peer, 2)
            remote(
                sent_there.at[0, peer_member, block_of(peer_block)],
                got_there.at[0, me], there_send.at[0], there_recv.at[0], (depth, peer),
            ).start()
            return 0

        lax.fori_loop(0, FAR, send, 0)
        lax.fori_loop(FAR + 1, LAT, send, 0)
        got_there[0, me] = sent_there[0, member, level]
        for load in loads[5:]:
            load.wait()
        for z in range(LEVELS):
            slow[z] = OMEGA * (slow[z] - ref_slow[z])
        edge_sent[0] = slow[LEVELS - 1]
        edge_sent[1] = slow[0]
        down = remote(edge_sent.at[0], edge_got.at[0], edge_send.at[0], edge_recv.at[0], (depth + 1, me))
        up = remote(edge_sent.at[1], edge_got.at[1], edge_send.at[1], edge_recv.at[1], (depth - 1, me))

        @pl.when(has_below)
        def _():
            down.start()

        @pl.when(has_above)
        def _():
            up.start()

        for z in range(LEVELS - 1):
            context[1, z + 1, 0] = slow[z]
            context[1, z, 1] = slow[z + 1]
        mine = ref_slow[0]
        for z in range(1, LEVELS):
            mine = jnp.where(level == z, ref_slow[z], mine)
        mult[0], mult[1] = multiplier(member, mine)
        nothing = jnp.zeros((ROWS, N), jnp.float32)

        @pl.when(has_above)
        def _():
            down.wait_recv()
            context[1, 0, 0] = edge_got[0]

        @pl.when(jnp.logical_not(has_above))
        def _():
            context[1, 0, 0] = nothing

        @pl.when(has_below)
        def _():
            up.wait_recv()
            context[1, LEVELS - 1, 1] = edge_got[1]

        @pl.when(jnp.logical_not(has_below))
        def _():
            context[1, LEVELS - 1, 1] = nothing

        holder = me // LEVELS
        place = lax.rem(me, LEVELS)
        for z in range(LEVELS):
            target = device_of(block_of(z), holder)

            @pl.when(target != me)
            def _():
                remote(
                    context.at[1, z], context.at[0, place], context_send, context_recv, (depth, target)
                ).start()

            @pl.when(target == me)
            def _():
                context[0, place] = context[1, z]

        @pl.when(jnp.logical_not(has_above))
        def _():
            target = device_of(0, holder)

            @pl.when(target != me)
            def _():
                remote(
                    source.at[0], source.at[1 + place], source_send, source_recv, (depth, target)
                ).start()

            @pl.when(target == me)
            def _():
                source[1 + place] = source[0]

    def later_there(tick):
        def send(step, _):
            peer = lax.bitwise_xor(member, GROUP - step)
            remote(
                sent_there.at[tick, peer], got_there.at[tick, pl.ds(LEVELS * member, LEVELS)],
                there_send.at[tick], there_recv.at[tick], (depth, device_of(block, peer)),
            ).start()
            return 0

        lax.fori_loop(1, GROUP, send, 0, unroll=True)
        got_there[tick, pl.ds(LEVELS * member, LEVELS)] = sent_there[tick, member]

    def far_member(to_block):
        across = (to_block // 2) != (block // 2)
        return jnp.where(to_block == block, 6, jnp.where(across, 2, 4))

    def group_back(tick):
        is_last = level == LEVELS - 1
        is_first = level == 0
        down_depth = depth + is_last.astype(jnp.int32)
        up_depth = depth - is_first.astype(jnp.int32)
        forth = jnp.where(flipped == 1, -1, 1)
        down_block = block + jnp.where(is_last, 0, forth)
        up_block = block - jnp.where(is_first, 0, forth)
        goes_down = jnp.logical_or(has_below, jnp.logical_not(is_last))
        goes_up = jnp.logical_or(has_above, jnp.logical_not(is_first))
        sides = (
            (0, goes_down, down_depth, down_block, far_member(down_block)),
            (1, goes_up, up_depth, up_block, far_member(up_block)),
        )

        def send(step, _):
            for side, goes, to_depth, to_block, far in sides:
                @pl.when(goes)
                def _():
                    peer = lax.bitwise_xor(member, lax.bitwise_xor(step, far))
                    remote(
                        sent_back.at[tick, pl.ds(LAT // 2 * side + 2 * peer, 2)],
                        got_back.at[tick, side, pl.ds(2 * member, 2)],
                        back_send.at[tick, side], back_recv.at[tick, side],
                        (to_depth, device_of(to_block, peer)),
                    ).start()

            return 0

        lax.fori_loop(0, GROUP, send, 0, unroll=True)
        return goes_down, goes_up

    def group_back_waits(tick, side):
        return remote(
            sent_back.at[tick, pl.ds(LAT // 2 * side, LAT // 2)], got_back.at[tick, side],
            back_send.at[tick, side], back_recv.at[tick, side], neighbour,
        )

    def last_waits(side, count, to):
        return remote(
            sent_back.at[last, pl.ds(0, count)], got_last.at[pl.ds(to, count)],
            last_send.at[side], last_recv.at[side], neighbour,
        )

    def one_tick(tick, _):
        real = state[0].reshape(HALF, N)
        imag = state[1].reshape(HALF, N)
        real, imag = along_y(real, imag, rows, -1)
        sent_there[tick] = to_tiles(real, imag, roll)

        @pl.when(tick == 0)
        def _():
            first_there()
            remote(
                got_there.at[0, pl.ds(0, LAT - 1)], got_there.at[0, pl.ds(0, LAT - 1)],
                there_send.at[0], there_recv.at[0], neighbour,
            ).wait_recv()

        @pl.when(tick > 0)
        def _():
            later_there(tick)
            remote(
                got_there.at[tick, pl.ds(0, LAT - LEVELS)],
                got_there.at[tick, pl.ds(0, LAT - LEVELS)],
                there_send.at[tick], there_recv.at[tick], neighbour,
            ).wait_recv()

        x = got_there[tick].reshape(N, LANES)
        x = middle(x, mult[0], mult[1], columns, roll).reshape(LAT, ROWS, LANES)

        @pl.when(tick < last)
        def _():
            pairs = x.reshape(LAT // 2, 2, ROWS, LANES)
            down, up = packed(pairs[:, 0], pairs[:, 1], roll)
            sent_back[tick, : LAT // 2] = down
            sent_back[tick, LAT // 2 :] = up
            goes = group_back(tick)

            def fill(which):
                angle = context[which, :, 0:2]
                corr[which, 0] = jnp.cos(angle)
                corr[which, 1] = jnp.sin(angle)

            @pl.when(tick == 0)
            def _():
                here = me // LEVELS == member
                for count in (LEVELS - 1, LEVELS):
                    @pl.when(here == (count < LEVELS))
                    def _():
                        remote(
                            context.at[1, pl.ds(0, count)], context.at[0, pl.ds(0, count)],
                            context_send, context_recv, neighbour,
                        ).wait_recv()

                    @pl.when(jnp.logical_and(jnp.logical_not(has_above), block == 0))
                    def _():
                        @pl.when(here == (count < LEVELS))
                        def _():
                            remote(
                                source.at[pl.ds(0, count)], source.at[pl.ds(1, count)],
                                source_send, source_recv, neighbour,
                            ).wait_recv()

                fill(0)

            @pl.when(tick == 1)
            def _():
                fill(1)

            comes_down = jnp.logical_or(has_above, level > 0)
            comes_up = jnp.logical_or(has_below, level < LEVELS - 1)
            for side, comes in ((0, comes_down), (1, comes_up)):
                @pl.when(comes)
                def _():
                    group_back_waits(tick, side).wait_recv()

                @pl.when(jnp.logical_not(comes))
                def _():
                    got_back[tick, side] = jnp.zeros((LAT // 2, ROWS, LANES), jnp.float32)

            down = got_back[tick, 0].reshape(GROUP, 2, ROWS, LANES)
            up = got_back[tick, 1].reshape(GROUP, 2, ROWS, LANES)
            for du, got in enumerate((down, up)):
                for part, piece in enumerate(from_pairs(got, roll)):
                    state[part, :, du] = piece
            for side in range(2):
                @pl.when(goes[side])
                def _():
                    group_back_waits(tick, side).wait_send()

        @pl.when(tick == last)
        def _():
            sent_back[last] = x
            slot = level * GROUP + member

            goes_down = jnp.logical_and(level == LEVELS - 1, has_below)
            goes_up = jnp.logical_and(level == 0, has_above)

            def send(step, _):
                peer = lax.bitwise_xor(me, lax.bitwise_xor(step, FAR))

                def push(side, where, place):
                    remote(
                        sent_back.at[last, peer], got_last.at[place],
                        last_send.at[side], last_recv.at[side], (where, peer),
                    ).start()

                @pl.when(goes_down)
                def _():
                    push(1, depth + 1, LAT + member)

                @pl.when(goes_up)
                def _():
                    push(2, depth - 1, LAT + GROUP + member)

                @pl.when(peer != me)
                def _():
                    push(0, depth, slot)

                return 0

            lax.fori_loop(0, LAT, send, 0)
            got_last[slot] = sent_back[last, me]
            for side, comes, place in ((1, has_above, LAT), (2, has_below, LAT + GROUP)):
                @pl.when(comes)
                def _():
                    last_waits(side, GROUP, place).wait_recv()

                @pl.when(jnp.logical_not(comes))
                def _():
                    got_last[pl.ds(place, GROUP)] = jnp.zeros((GROUP, ROWS, LANES), jnp.float32)

            last_waits(0, LAT - 1, 0).wait_recv()
            down = is_down((GROUP, ROWS, LANES))
            for z in range(LEVELS):
                above = GROUP * (z - 1) if z > 0 else LAT
                below = GROUP * (z + 1) if z < LEVELS - 1 else LAT + GROUP
                got = jnp.where(down, got_last[above : above + GROUP], got_last[below : below + GROUP])
                for n, piece in enumerate(from_tiles(got, roll)):
                    state[n // 2, z, n % 2] = piece
            last_waits(0, LAT - 1, 0).wait_send()
            for side, goes in ((1, goes_down), (2, goes_up)):
                @pl.when(goes)
                def _():
                    last_waits(side, LAT, 0).wait_send()

        real, imag = along_y(state[0].reshape(HALF, N), state[1].reshape(HALF, N), rows, 1)
        real = real.reshape(LEVELS, 2, ROWS, N)
        imag = imag.reshape(LEVELS, 2, ROWS, N)
        at_end = (tick == last).astype(jnp.int32)
        for g in range(LEVELS):
            heads = jnp.logical_and(jnp.logical_not(has_above), jnp.where(tick == last, g, level) == 0)
            tails = jnp.logical_and(
                jnp.logical_not(has_below), jnp.where(tick == last, g, level) == LEVELS - 1
            )
            origin = source[jnp.where(tick == last, 0, 1 + g)]
            parts = mixed(
                real[g], imag[g], corr[at_end, :, g], context[at_end, g, 2], heads, tails, origin
            )
            for part in range(2):
                state[part, g, 0], state[part, g, 1] = parts[part]
        return 0

    lax.fori_loop(0, TICKS, one_tick, 0)
    remote(
        got_there.at[0, pl.ds(0, LAT - 1)], got_there.at[0, pl.ds(0, LAT - 1)],
        there_send.at[0], there_recv.at[0], neighbour,
    ).wait_send()
    for tick in range(1, TICKS):
        remote(
            got_there.at[tick, pl.ds(0, LAT - LEVELS)], got_there.at[tick, pl.ds(0, LAT - LEVELS)],
            there_send.at[tick], there_recv.at[tick], neighbour,
        ).wait_send()
    holder = me // LEVELS
    here = holder == member
    for count in (LEVELS - 1, LEVELS):
        @pl.when(here == (count < LEVELS))
        def _():
            remote(
                context.at[1, pl.ds(0, count)], context.at[0, pl.ds(0, count)],
                context_send, context_recv, neighbour,
            ).wait_send()

    @pl.when(jnp.logical_and(jnp.logical_not(has_above), device_of(0, holder) != me))
    def _():
        remote(source.at[0], source.at[1], source_send, source_recv, neighbour).wait_send()

    for side, goes in ((0, has_below), (1, has_above)):
        @pl.when(goes)
        def _():
            remote(
                edge_sent.at[side], edge_got.at[side], edge_send.at[side], edge_recv.at[side], neighbour
            ).wait_send()


def handed_out(state, out_dr, out_di, out_ur, out_ui, sems):
    copies = [
        pltpu.make_async_copy(state.at[n % 2, :, n // 2], out, sems.at[n])
        for n, out in enumerate((out_dr, out_di, out_ur, out_ui))
    ]
    for copy in copies:
        copy.start()
    for copy in copies:
        copy.wait()


def solution(mesh):
    tables = constants()
    plane = jax.ShapeDtypeStruct((LEVELS, ROWS, N), jnp.float32)
    anywhere = pl.BlockSpec(memory_space=pl.ANY)
    smem = pl.BlockSpec(memory_space=pltpu.SMEM)
    whole = pl.BlockSpec(memory_space=pltpu.VMEM)
    f32 = jnp.float32

    def step(*args):
        state = pl.pallas_call(
            kernel,
            out_shape=pltpu.VMEM((2, LEVELS, 2, ROWS, N), f32),
            in_specs=[anywhere] * 5 + [smem] + [anywhere] * 5,
            out_specs=whole,
            scratch_shapes=[
                pltpu.VMEM((LEVELS, ROWS, N), f32),
                pltpu.VMEM((1 + LEVELS, 2, ROWS, N), f32),
                *[pltpu.VMEM(table.shape, jnp.bfloat16) for table in tables],
                pltpu.VMEM((2, N, LANES), f32),
                pltpu.VMEM((2, LEVELS, 3, ROWS, N), f32),
                pltpu.VMEM((2, 2, LEVELS, 2, ROWS, N), f32),
                pltpu.VMEM((TICKS, GROUP, LEVELS, ROWS, LANES), f32),
                pltpu.VMEM((TICKS, LAT, ROWS, LANES), f32),
                pltpu.VMEM((TICKS, LAT, ROWS, LANES), f32),
                pltpu.VMEM((TICKS - 1, 2, LAT // 2, ROWS, LANES), f32),
                pltpu.VMEM((LAT + 2 * GROUP, ROWS, LANES), f32),
                *[pltpu.VMEM((2, ROWS, N), f32)] * 2,
                pltpu.SemaphoreType.DMA((10,)),
                *[pltpu.SemaphoreType.DMA((TICKS,))] * 2,
                *[pltpu.SemaphoreType.DMA((TICKS - 1, 2))] * 2,
                *[pltpu.SemaphoreType.DMA((3,))] * 2,
                *[pltpu.SemaphoreType.DMA((2,))] * 2,
                *[pltpu.SemaphoreType.DMA] * 4,
            ],
            compiler_params=pltpu.CompilerParams(collective_id=0, has_side_effects=True),
        )(*args, *[jnp.asarray(table) for table in tables])
        return pl.pallas_call(
            handed_out,
            out_shape=[plane] * 4,
            in_specs=[whole],
            out_specs=[anywhere] * 4,
            scratch_shapes=[pltpu.SemaphoreType.DMA((4,))],
            compiler_params=pltpu.CompilerParams(vmem_limit_bytes=2**20),
        )(state)

    lateral = P("depth", "lat", None)
    return jax.shard_map(
        step,
        mesh=mesh,
        in_specs=(lateral,) * 5 + (P("depth"), lateral, P("lat", None), P("lat", None)),
        out_specs=(lateral,) * 4,
        check_vma=False,
    )
```
